128 devices in a mesh: row: 8 (over y_lo, z), col: 16 (over x, y_hi, core).
Axes of the slice: x: 4, y: 4 (y_hi: 2, y_lo: 2; y = y_hi * 2 + y_lo), z: 4, core: 2. Of those that a mesh axis runs over, the one named last changes fastest.
Arguments:
- inputs: bfloat16 [1024, 8192], P('row', 'col'), may hold values from -6 to 6
- gate_matrix: bfloat16 [8192, 26624], P('col', 'row'), may hold values from -0.0625 to 0.0625
- lift_matrix: bfloat16 [8192, 26624], P('col', 'row'), may hold values from -0.0625 to 0.0625
- out_cotangent: bfloat16 [1024, 26624], P('col', 'row'), may hold values from -6 to 6
Outputs:
- gated_out: bfloat16 [1024, 26624], P('col', 'row')
- grad_inputs: bfloat16 [1024, 8192], P('row', 'col')
- grad_gate: bfloat16 [8192, 26624], P('col', 'row')
- grad_lift: bfloat16 [8192, 26624], P('col', 'row')
The draws below stay inside these ranges and needn't reach their ends.
All inputs are finite; a program needn't handle non-finite values.
Results may differ from the reference program's by a relative error of at most 0.0049.
Values may be sent and summed in bfloat16 or wider, within the bound.
No kernel may reach another device: no remote copies, remote signals or barrier semaphores. Data moves between devices by JAX's collectives and lax.ppermute only.
A program may use at most 192 MiB of HBM per device.

```python
import jax
import jax.numpy as jnp

D = 8192
FF = 26624
TOKENS = 1024


def shard_levels(key, extent, shards, smallest, top_value):
    def one(dim, blocks):
        steps = jax.random.uniform(jax.random.fold_in(jax.random.fold_in(key, 6), dim), (blocks,), jnp.float32, smallest / len(shards), top_value / len(shards))
        return jnp.repeat(jnp.exp(steps), extent[dim] // blocks).reshape((-1,) + (1,) * (len(extent) - dim - 1))

    gain = one(*shards[0])
    for cut in shards[1:]:
        gain = gain * one(*cut)
    return gain


def gaussian(own_key, extent, spread, reach, shards=(), held_as=jnp.bfloat16):
    entries = spread * jax.random.normal(own_key, extent, jnp.float32)
    if shards:
        entries = entries * shard_levels(own_key, extent, shards, -0.22, 0.18)
    return jnp.clip(entries, -reach, reach).astype(held_as)


def setup_inputs(seed: int = 0) -> dict:
    key_of = jax.random.split(jax.random.key(seed), 5)
    inputs = gaussian(key_of[0], (TOKENS, D), 1.0, 6.0, ((0, 8), (1, 16)))
    gate_matrix = gaussian(key_of[1], (D, FF), D ** -0.5, 0.0625, ((0, 16), (1, 8)))
    lift_matrix = gaussian(key_of[2], (D, FF), D ** -0.5, 0.0625, ((0, 16), (1, 8)))
    out_cotangent = gaussian(key_of[3], (TOKENS, FF), 1.0, 6.0, ((0, 16), (1, 8)))
    return dict(inputs=inputs, gate_matrix=gate_matrix, lift_matrix=lift_matrix, out_cotangent=out_cotangent)


def reference(inputs, gate_matrix, lift_matrix, out_cotangent):
    gate = jnp.dot(inputs, gate_matrix, preferred_element_type=jnp.float32)
    lift = jnp.dot(inputs, lift_matrix, preferred_element_type=jnp.float32)
    sigma = jax.nn.sigmoid(gate)
    silu_val = gate * sigma
    gated_out = (silu_val * lift).astype(jnp.bfloat16)
    cot = out_cotangent.astype(jnp.float32)
    grad_gatepre = (cot * lift * sigma * (1.0 + gate * (1.0 - sigma))).astype(jnp.bfloat16)
    grad_liftpre = (cot * silu_val).astype(jnp.bfloat16)
    grad_inputs = jnp.dot(grad_gatepre, gate_matrix.T, preferred_element_type=jnp.float32) + jnp.dot(grad_liftpre, lift_matrix.T, preferred_element_type=jnp.float32)
    grad_gate = jnp.dot(inputs.T, grad_gatepre, preferred_element_type=jnp.float32)
    grad_lift = jnp.dot(inputs.T, grad_liftpre, preferred_element_type=jnp.float32)
    return (gated_out, grad_inputs.astype(jnp.bfloat16), grad_gate.astype(jnp.bfloat16), grad_lift.astype(jnp.bfloat16))
```

```python
import functools

import jax
import jax.numpy as jnp
from jax import lax
from jax.experimental import pallas as pl
from jax.experimental.pallas import tpu as pltpu
from jax.sharding import PartitionSpec as P

F32, BF16 = jnp.float32, jnp.bfloat16
TILE = 256
CHUNKS = (("a", 4), ("b", 3), ("a", 3), ("b", 3))
MIB = 1 << 20


def column(x, y, core):
    return (x % 4) * 4 + (y % 2) * 2 + core % 2


COLS = [(c, c // 4, (c // 2) % 2, c % 2) for c in range(16)]
CORE = [(c, column(x, y, k + 1)) for c, x, y, k in COLS]
ALONG_Y = [(c, column(x, y + 1, k)) for c, x, y, k in COLS]
ALONG_X = [(c, column(x + 1 - 2 * k, y, k)) for c, x, y, k in COLS]


def row_step(i):
    return [(r, ((r // 4 + i // 4) % 2) * 4 + (r % 4 + i % 4) % 4) for r in range(8)]


def over_x(v):
    return lax.ppermute(v, "col", ALONG_X)


def over_y(v):
    return lax.ppermute(v, "col", ALONG_Y)


def over_core(v):
    return lax.ppermute(v, "col", CORE)


def params(mib):
    return pltpu.CompilerParams(vmem_limit_bytes=mib * MIB)


def whole(shape):
    return pl.BlockSpec(shape, lambda *_: (0,) * len(shape))


SMEM = pl.BlockSpec(memory_space=pltpu.SMEM)
ANY = pl.BlockSpec(memory_space=pl.ANY)


def cost(flops, bytes_accessed):
    return pl.CostEstimate(flops=flops, bytes_accessed=bytes_accessed, transcendentals=0)


def arrange_kernel(at_ref, own_ref, sib_ref, lhs_ref, xt_ref):
    def piece(ref, i):
        return ref[at_ref[0, i], pl.ds(pl.multiple_of(at_ref[1, i], 64), 64), :]

    for i in range(8):
        lhs_ref[pl.ds(64 * i, 64), :512] = piece(own_ref, i)
        lhs_ref[pl.ds(64 * i, 64), 512:] = piece(sib_ref, i)
    for i in range(8):
        pair = [piece(own_ref, 8 + 2 * i), piece(own_ref, 9 + 2 * i)]
        xt_ref[:, pl.ds(128 * i, 128)] = jnp.concatenate(pair, axis=0).T


def arrange(at, own, sib):
    return pl.pallas_call(
        arrange_kernel,
        out_shape=(jax.ShapeDtypeStruct((512, 1024), BF16), jax.ShapeDtypeStruct((512, 1024), BF16)),
        in_specs=[SMEM, whole(own.shape), whole(own.shape)],
        out_specs=(whole((512, 1024)), whole((512, 1024))),
        grid=(1,),
        compiler_params=params(16),
        cost_estimate=cost(0, 4 * MIB),
        name="arrange_tokens",
    )(at, own, sib)


def forward_kernel(path, lhs_ref, go_ref, gs_ref, lo_ref, ls_ref, *outs):
    a, b = lhs_ref[:, :512], lhs_ref[:, 512:]
    for m, (o, s) in enumerate(((go_ref, gs_ref), (lo_ref, ls_ref))):
        p = jnp.dot(a, o[...], preferred_element_type=F32)
        p = p + jnp.dot(b, s[...], preferred_element_type=F32)
        for g in range(4):
            for dy in range(2):
                q = p[g * 128 + dy * 64 : g * 128 + dy * 64 + 64]
                if path == "a":
                    outs[g][dy, m] = q.astype(outs[g].dtype)
                else:
                    outs[dy][g, m] = q.astype(outs[dy].dtype)


def forward(path, first, tiles, lhs, own_gate, sib_gate, own_lift, sib_lift):
    n = tiles * TILE
    if path == "a":
        lead, kinds = 2, (BF16, BF16, F32, F32)
    else:
        lead, kinds = 4, (F32, BF16)
    w = pl.BlockSpec((512, TILE), lambda j: (0, first + j))
    return pl.pallas_call(
        functools.partial(forward_kernel, path),
        out_shape=tuple(jax.ShapeDtypeStruct((lead, 2, 64, n), t) for t in kinds),
        in_specs=[whole((512, 1024)), w, w, w, w],
        out_specs=tuple(pl.BlockSpec((lead, 2, 64, TILE), lambda j: (0, 0, 0, j)) for _ in kinds),
        grid=(tiles,),
        compiler_params=params(24),
        cost_estimate=cost(4 * 512 * 1024 * n, 4 * 1024 * n + 6 * 1024 * n),
        name="forward_" + path,
    )(lhs, own_gate, sib_gate, own_lift, sib_lift)


def gate_kernel(terms, *refs):
    total = refs[0][...].astype(F32)
    for ref in refs[1:terms]:
        total = total + ref[...].astype(F32)
    cot = refs[terms][...].astype(F32)
    gated_ref, grads_ref = refs[-2:]
    gate, lift = total[0], total[1]
    sigma = jax.nn.sigmoid(gate)
    silu = gate * sigma
    gated_ref[...] = (silu * lift).astype(BF16)
    grads_ref[0] = (cot * lift * sigma * (1.0 + gate * (1.0 - sigma))).astype(BF16)
    grads_ref[1] = (cot * silu).astype(BF16)


def gating(first, tiles, terms, cot, gated):
    n = tiles * TILE
    wide = pl.BlockSpec((64, TILE), lambda j: (0, first + j))
    part = pl.BlockSpec((2, 64, TILE), lambda j: (0, 0, j))
    more, alias = ([], {}) if gated is None else ([gated], {len(terms) + 1: 0})
    return pl.pallas_call(
        functools.partial(gate_kernel, len(terms)),
        out_shape=(jax.ShapeDtypeStruct(cot.shape, BF16), jax.ShapeDtypeStruct((2, 64, n), BF16)),
        in_specs=[part] * len(terms) + [wide] + [ANY] * len(more),
        out_specs=(wide, part),
        grid=(tiles,),
        input_output_aliases=alias,
        compiler_params=params(16),
        cost_estimate=cost(0, 64 * n * 20),
        name="gating",
    )(*terms, cot, *more)


def backward_kernel(path, pieces, do_w, do_y, carried, *refs):
    refs = list(refs)
    held = [refs.pop(0) for _ in range(pieces)]
    if do_w:
        xt_ref = refs.pop(0)
    if do_y:
        w_refs = [refs.pop(0), refs.pop(0)]
        if carried:
            y_in = refs.pop(0)
    outs = refs[-(2 * do_w + do_y):]
    if do_y:
        y_ref = outs[-1]

        @pl.when(pl.program_id(0) == 0)
        def _():
            y_ref[...] = y_in[...] if carried else jnp.zeros_like(y_ref)

    both = []
    for m in range(2):
        rows = []
        for dy in range(2):
            for q in range(8):
                if path == "a":
                    rows.append(held[q][dy, m])
                else:
                    rows.append(held[2 * (q // 4) + dy][q % 4, m])
        both.append(jnp.concatenate(rows, axis=0))
    if do_w:
        for m in range(2):
            outs[m][...] = jnp.dot(xt_ref[...], both[m], preferred_element_type=F32).astype(BF16)
    if do_y:
        dims = (((1,), (1,)), ((), ()))
        add = lax.dot_general(both[0], w_refs[0][...], dims, preferred_element_type=F32)
        add = add + lax.dot_general(both[1], w_refs[1][...], dims, preferred_element_type=F32)
        y_ref[...] += add


def backward(path, first, tiles, pieces, xt, gate, lift, grads, y, do_w, do_y):
    n = tiles * TILE
    lead = pieces[0].shape[0]
    wide = pl.BlockSpec((512, TILE), lambda j: (0, first + j))
    args = list(pieces)
    specs = [pl.BlockSpec((lead, 2, 64, TILE), lambda j: (0, 0, 0, j))] * len(pieces)
    alias, shapes, out_specs = {}, [], []
    if do_w:
        args.append(xt)
        specs.append(whole(xt.shape))
        shapes += [jax.ShapeDtypeStruct(gate.shape, BF16)] * 2
        out_specs += [wide, wide]
    if do_y:
        args += [gate, lift]
        specs += [wide, wide]
        if y is not None:
            alias[len(args)] = len(shapes)
            args.append(y)
            specs.append(whole((1024, 512)))
        shapes.append(jax.ShapeDtypeStruct((1024, 512), F32))
        out_specs.append(whole((1024, 512)))
    if do_w and grads is not None:
        for m in range(2):
            alias[len(args)] = m
            args.append(grads[m])
            specs.append(ANY)
    out = pl.pallas_call(
        functools.partial(backward_kernel, path, len(pieces), do_w, do_y, y is not None),
        out_shape=tuple(shapes),
        in_specs=specs,
        out_specs=tuple(out_specs),
        grid=(tiles,),
        input_output_aliases=alias,
        compiler_params=params(40),
        cost_estimate=cost((do_w + do_y) * 4 * 512 * 1024 * n, 8 * 1024 * n + 4 * MIB),
        name="backward_" + path,
    )(*args)
    return (tuple(out[:2]) if do_w else grads), (out[-1] if do_y else y)


def split_kernel(at_ref, y_ref, own_ref, *outs):
    for i in range(8):
        for h in range(2):
            rows = y_ref[pl.ds(pl.multiple_of(at_ref[i, h], 64), 64), :]
            if i == 0:
                own_ref[pl.ds(64 * h, 64), :] = rows
            else:
                outs[i - 1][pl.ds(64 * h, 64), :] = rows.astype(BF16)


def split(at, y):
    kinds = [F32] + [BF16] * 7
    return pl.pallas_call(
        split_kernel,
        out_shape=tuple(jax.ShapeDtypeStruct((128, 512), t) for t in kinds),
        in_specs=[SMEM, whole((1024, 512))],
        out_specs=tuple(whole((128, 512)) for _ in kinds),
        grid=(1,),
        compiler_params=params(16),
        cost_estimate=cost(0, 3 * MIB),
        name="split_rows",
    )(at, y)


def body(inputs, gate_matrix, lift_matrix, out_cotangent):
    r, c = lax.axis_index("row"), lax.axis_index("col")
    x, yh, k = c // 4, (c // 2) % 2, c % 2
    yl, z = r // 4, r % 4

    sib_gate, sib_lift = over_core(gate_matrix), over_core(lift_matrix)
    blocks = [inputs] + [lax.ppermute(inputs, "row", row_step(i)) for i in range(1, 8)]
    own_x = jnp.stack(blocks)
    sib_x = over_core(own_x)

    def held_at(dx, dy):
        block = 2 * ((x + dx) % 4) + (yh + dy) % 2
        return ((yl - block // 4) % 2) * 4 + (z - block % 4) % 4

    fwd = [(2, k), (1 + 2 * k, 1 - k), (1 + 2 * k, k), (0, k)]
    bwd = [(0, k), (3 - 2 * k, k), (3 - 2 * k, 1 - k), (2, k)]
    bwd += [(0, 1 - k), (1 + 2 * k, 1 - k), (1 + 2 * k, k), (2, 1 - k)]
    order = [(held_at(dx, dy), 64 * h) for dx, h in fwd for dy in range(2)]
    order += [(held_at(dx, dy), 64 * h) for dy in range(2) for dx, h in bwd]
    at = jnp.stack([jnp.stack([i for i, _ in order]), jnp.stack([h for _, h in order])]).astype(jnp.int32)
    lhs, xt = arrange(at, own_x, sib_x)

    gated, grads, y = None, None, None
    first, todo = 0, []
    for path, tiles in CHUNKS:
        products = forward(path, first, tiles, lhs, gate_matrix, sib_gate, lift_matrix, sib_lift)
        if path == "a":
            far, near_o, near_k, own = products
        else:
            keep, send = products
            near = keep + over_y(send).astype(F32)
            far, near_o, near_k, own = near[0].astype(BF16), near[1].astype(BF16), near[2], near[3]
        got_far = over_x(far)
        got_o = over_core(over_x(near_o))
        got_k = over_x((near_k + got_far.astype(F32)).astype(BF16))
        if path == "a":
            total = own + got_k.astype(F32) + got_o.astype(F32)
            terms = [total[0], over_y(total[1].astype(BF16))]
        else:
            terms = [own, got_k, got_o]
        gated, own = gating(first, tiles, terms, out_cotangent, gated)

        if path == "a":
            own = jnp.stack([own, over_y(own)])
        sib = over_core(own)
        near_k = over_x(own)
        near_o = over_x(sib)
        far = over_x(near_k)
        if path == "a":
            pieces = [own, near_k, near_o, far]
            pieces = pieces + [sib] + [over_core(v) for v in pieces[1:]]
        else:
            here = jnp.stack([own, near_k, near_o, far])
            there = over_y(here)
            pieces = [here, there, over_core(here), over_core(there)]
        todo.append((path, first, tiles, pieces))
        first += tiles

    for i, (path, first, tiles, pieces) in enumerate(todo):
        rest = (xt, gate_matrix, lift_matrix)
        if i + 1 < len(todo):
            grads, y = backward(path, first, tiles, pieces, *rest, grads, y, True, True)
        else:
            _, y = backward(path, first, tiles, pieces, *rest, None, y, False, True)
            grads, _ = backward(path, first, tiles, pieces, *rest, grads, None, True, False)

    def place(i, h):
        block = ((yl + i // 4) % 2) * 4 + (z + i % 4) % 4
        dx, dy = (block // 2 - x) % 4, (block - yh) % 2
        same = (h == k).astype(jnp.int32)
        q = jnp.where(dx == 0, 4 - 4 * same, jnp.where(dx == 2, 7 - 4 * same, jnp.where(dx == 3 - 2 * k, 2 - same, 5 + same)))
        return 64 * (8 * dy + q)

    where = jnp.stack([jnp.stack([place(i, h) for h in range(2)]) for i in range(8)]).astype(jnp.int32)
    parts = split(where, y)
    total = parts[0]
    for i in range(1, 8):
        total = total + lax.ppermute(parts[i], "row", row_step(i)).astype(F32)
    return (gated, total.astype(BF16), grads[0], grads[1])


def solution(mesh):
    return jax.shard_map(
        body,
        mesh=mesh,
        in_specs=(P("row", "col"), P("col", "row"), P("col", "row"), P("col", "row")),
        out_specs=(P("col", "row"), P("row", "col"), P("col", "row"), P("col", "row")),
        check_vma=False,
    )
```

```python
import functools

import jax
import jax.numpy as jnp
from jax import lax
from jax.experimental import pallas as pl
from jax.experimental.pallas import tpu as pltpu
from jax.sharding import PartitionSpec as P

F32, BF16 = jnp.float32, jnp.bfloat16
TILE = 256
CHUNKS = (("b", 3), ("a", 4), ("a", 3), ("b", 3))
ORDER = (
    (0, "f"), (1, "f"), (3, "f"), (1, "a1"), (0, "b1"), (2, "f"), (1, "ac"), (0, "b2"),
    (1, "a2"), (2, "a1"), (0, "bc"), (3, "b1"), (0, "g"), (1, "g"), (0, "c1"), (2, "ac"),
    (3, "b2"), (2, "a2"), (0, "c2"), (1, "b1"), (1, "b2"), (3, "bc"), (2, "g"), (3, "g"),
    (0, "c3"), (2, "b1"), (3, "c1"), (1, "b3"), (3, "c2"), (1, "b4"), (2, "b2"), (3, "c3"),
    (0, "c4"), (1, "d"), (1, "K"), (2, "b3"), (0, "d"), (0, "K"), (2, "b4"), (3, "c4"),
    (2, "d"), (2, "K"), (3, "d"), (3, "Ky"), (3, "Kw"),
)
MIB = 1 << 20


def column(x, y, core):
    return (x % 4) * 4 + (y % 2) * 2 + core % 2


COLS = [(c, c // 4, (c // 2) % 2, c % 2) for c in range(16)]
CORE = [(c, column(x, y, k + 1)) for c, x, y, k in COLS]
ALONG_Y = [(c, column(x, y + 1, k)) for c, x, y, k in COLS]
ALONG_X = [(c, column(x + 1 - 2 * k, y, k)) for c, x, y, k in COLS]


def row_step(i):
    return [(r, ((r // 4 + i // 4) % 2) * 4 + (r % 4 + i % 4) % 4) for r in range(8)]


def over_x(v):
    return lax.ppermute(v, "col", ALONG_X)


def over_y(v):
    return lax.ppermute(v, "col", ALONG_Y)


def over_core(v):
    return lax.ppermute(v, "col", CORE)


def params(mib):
    return pltpu.CompilerParams(vmem_limit_bytes=mib * MIB)


def whole(shape):
    return pl.BlockSpec(shape, lambda *_: (0,) * len(shape))


SMEM = pl.BlockSpec(memory_space=pltpu.SMEM)
ANY = pl.BlockSpec(memory_space=pl.ANY)


def cost(flops, bytes_accessed):
    return pl.CostEstimate(flops=flops // 1000, bytes_accessed=bytes_accessed // 1000, transcendentals=0)


def arrange_kernel(at_ref, own_ref, sib_ref, lhs_ref, xt_ref):
    def piece(ref, i):
        return ref[at_ref[0, i], pl.ds(pl.multiple_of(at_ref[1, i], 64), 64), :]

    for i in range(8):
        lhs_ref[pl.ds(64 * i, 64), :512] = piece(own_ref, i)
        lhs_ref[pl.ds(64 * i, 64), 512:] = piece(sib_ref, i)
    for i in range(8):
        pair = [piece(own_ref, 8 + 2 * i), piece(own_ref, 9 + 2 * i)]
        xt_ref[:, pl.ds(128 * i, 128)] = jnp.concatenate(pair, axis=0).T


def arrange(at, own, sib):
    return pl.pallas_call(
        arrange_kernel,
        out_shape=(jax.ShapeDtypeStruct((512, 1024), BF16), jax.ShapeDtypeStruct((512, 1024), BF16)),
        in_specs=[SMEM, whole(own.shape), whole(own.shape)],
        out_specs=(whole((512, 1024)), whole((512, 1024))),
        grid=(1,),
        compiler_params=params(16),
        cost_estimate=cost(0, 4 * MIB),
        name="arrange_tokens",
    )(at, own, sib)


def forward_kernel(path, lhs_ref, go_ref, gs_ref, lo_ref, ls_ref, *outs):
    a, b = lhs_ref[:, :512], lhs_ref[:, 512:]
    for m, (o, s) in enumerate(((go_ref, gs_ref), (lo_ref, ls_ref))):
        p = jnp.dot(a, o[...], preferred_element_type=F32)
        p = p + jnp.dot(b, s[...], preferred_element_type=F32)
        for g in range(4):
            for dy in range(2):
                q = p[g * 128 + dy * 64 : g * 128 + dy * 64 + 64]
                if path == "a":
                    outs[g][dy, m] = q.astype(outs[g].dtype)
                else:
                    outs[dy][g, m] = q.astype(outs[dy].dtype)


def forward(path, first, tiles, lhs, own_gate, sib_gate, own_lift, sib_lift):
    n = tiles * TILE
    if path == "a":
        lead, kinds = 2, (BF16, BF16, F32, F32)
    else:
        lead, kinds = 4, (F32, BF16)
    w = pl.BlockSpec((512, TILE), lambda j: (0, first + j))
    return pl.pallas_call(
        functools.partial(forward_kernel, path),
        out_shape=tuple(jax.ShapeDtypeStruct((lead, 2, 64, n), t) for t in kinds),
        in_specs=[whole((512, 1024)), w, w, w, w],
        out_specs=tuple(pl.BlockSpec((lead, 2, 64, TILE), lambda j: (0, 0, 0, j)) for _ in kinds),
        grid=(tiles,),
        compiler_params=params(24),
        cost_estimate=cost(4 * 512 * 1024 * n, 4 * 1024 * n + 6 * 1024 * n),
        name="forward_" + path,
    )(lhs, own_gate, sib_gate, own_lift, sib_lift)


def gate_kernel(terms, *refs):
    total = refs[0][...].astype(F32)
    for ref in refs[1:terms]:
        total = total + ref[...].astype(F32)
    cot = refs[terms][...].astype(F32)
    gated_ref, grads_ref = refs[-2:]
    gate, lift = total[0], total[1]
    sigma = jax.nn.sigmoid(gate)
    silu = gate * sigma
    gated_ref[...] = (silu * lift).astype(BF16)
    grads_ref[0] = (cot * lift * sigma * (1.0 + gate * (1.0 - sigma))).astype(BF16)
    grads_ref[1] = (cot * silu).astype(BF16)


def gating(first, tiles, terms, cot, gated):
    n = tiles * TILE
    wide = pl.BlockSpec((64, TILE), lambda j: (0, first + j))
    part = pl.BlockSpec((2, 64, TILE), lambda j: (0, 0, j))
    more, alias = ([], {}) if gated is None else ([gated], {len(terms) + 1: 0})
    return pl.pallas_call(
        functools.partial(gate_kernel, len(terms)),
        out_shape=(jax.ShapeDtypeStruct(cot.shape, BF16), jax.ShapeDtypeStruct((2, 64, n), BF16)),
        in_specs=[part] * len(terms) + [wide] + [ANY] * len(more),
        out_specs=(wide, part),
        grid=(tiles,),
        input_output_aliases=alias,
        compiler_params=params(16),
        cost_estimate=cost(0, 64 * n * 20),
        name="gating",
    )(*terms, cot, *more)


def backward_kernel(arrays, table, do_w, do_y, carried, *refs):
    refs = list(refs)
    held = [refs.pop(0) for _ in range(arrays)]
    if do_w:
        xt_ref = refs.pop(0)
    if do_y:
        w_refs = [refs.pop(0), refs.pop(0)]
        if carried:
            y_in = refs.pop(0)
    outs = refs[-(2 * do_w + do_y) :]
    if do_y:
        y_ref = outs[-1]

        @pl.when(pl.program_id(0) == 0)
        def _():
            y_ref[...] = y_in[...] if carried else jnp.zeros_like(y_ref)

    both = [jnp.concatenate([held[i][j, m] for i, j in table], axis=0) for m in range(2)]
    if do_w:
        for m in range(2):
            outs[m][...] = jnp.dot(xt_ref[...], both[m], preferred_element_type=F32).astype(BF16)
    if do_y:
        dims = (((1,), (1,)), ((), ()))
        add = lax.dot_general(both[0], w_refs[0][...], dims, preferred_element_type=F32)
        add = add + lax.dot_general(both[1], w_refs[1][...], dims, preferred_element_type=F32)
        y_ref[...] += add


def backward(first, tiles, pieces, table, xt, gate, lift, grads, y, do_w, do_y):
    n = tiles * TILE
    wide = pl.BlockSpec((512, TILE), lambda j: (0, first + j))
    args = list(pieces)
    specs = [pl.BlockSpec((v.shape[0], 2, 64, TILE), lambda j: (0, 0, 0, j)) for v in pieces]
    alias, shapes, out_specs = {}, [], []
    if do_w:
        args.append(xt)
        specs.append(whole(xt.shape))
        shapes += [jax.ShapeDtypeStruct(gate.shape, BF16)] * 2
        out_specs += [wide, wide]
    if do_y:
        args += [gate, lift]
        specs += [wide, wide]
        if y is not None:
            args.append(y)
            specs.append(whole((1024, 512)))
        shapes.append(jax.ShapeDtypeStruct((1024, 512), F32))
        out_specs.append(whole((1024, 512)))
    if do_w and grads is not None:
        for m in range(2):
            alias[len(args)] = m
            args.append(grads[m])
            specs.append(ANY)
    out = pl.pallas_call(
        functools.partial(backward_kernel, len(pieces), table, do_w, do_y, y is not None),
        out_shape=tuple(shapes),
        in_specs=specs,
        out_specs=tuple(out_specs),
        grid=(tiles,),
        input_output_aliases=alias,
        compiler_params=params(28),
        cost_estimate=cost((do_w + do_y) * 4 * 512 * 1024 * n, 8 * 1024 * n + 4 * MIB),
        name="backward",
    )(*args)
    return (tuple(out[:2]) if do_w else grads), (out[-1] if do_y else y)


def split_kernel(at_ref, y_ref, own_ref, *outs):
    for i in range(8):
        for h in range(2):
            rows = y_ref[pl.ds(pl.multiple_of(at_ref[i, h], 64), 64), :]
            if i == 0:
                own_ref[pl.ds(64 * h, 64), :] = rows
            else:
                outs[i - 1][pl.ds(64 * h, 64), :] = rows.astype(BF16)


def split(at, y):
    kinds = [F32] + [BF16] * 7
    return pl.pallas_call(
        split_kernel,
        out_shape=tuple(jax.ShapeDtypeStruct((128, 512), t) for t in kinds),
        in_specs=[SMEM, whole((1024, 512))],
        out_specs=tuple(whole((128, 512)) for _ in kinds),
        grid=(1,),
        compiler_params=params(16),
        cost_estimate=cost(0, 3 * MIB),
        name="split_rows",
    )(at, y)


class Sequence:
    def __init__(self):
        self.last = None

    def __call__(self, *values):
        if self.last is not None:
            *values, self.last = lax.optimization_barrier((*values, self.last))
        return values[0] if len(values) == 1 else values

    def done(self, value):
        self.last = value


def x_first(seq, first, tiles, use):
    s = {}
    n = tiles * TILE

    def products():
        s["far"], s["near_o"], s["near_k"], s["own"] = forward("a", first, tiles, seq(use["lhs"]), *use["weights"])
        seq.done(s["near_k"])
        s["far"] = over_x(s["far"])

    def relay():
        far, near_k, near_o = seq(s["far"], s["near_k"], s["near_o"])
        near = jnp.stack([(near_k + far.astype(F32)).astype(BF16), near_o])
        seq.done(near)
        s["near"] = over_x(near)

    def swap():
        s["near"] = seq(s["near"])
        other = s["near"][1]
        seq.done(other)
        s["other"] = over_core(other)

    def sum_x():
        near, other, own = seq(s["near"], s["other"], s["own"])
        total = own + near[0].astype(F32) + other.astype(F32)
        send = total[1].astype(BF16)
        seq.done(send)
        s["own"], s["other"] = total[0], over_y(send)

    def gate():
        own, other = seq(s["own"], s["other"])
        use["gated"], s["own"] = gating(first, tiles, [own, other], use["cot"], use["gated"])
        seq.done(s["own"])
        s["other"] = over_y(s["own"])

    def spread():
        own, other = seq(s["own"], s["other"])
        s["own"] = jnp.stack([own, other])
        seq.done(s["own"])
        s["sib"] = over_core(s["own"])

    def spread_x():
        own, sib = seq(s["own"], s["sib"])
        s["full"] = jnp.stack([own, sib])
        seq.done(s["full"])
        s["near"] = over_x(s["full"])

    def pass_on():
        s["near"] = seq(s["near"])
        far = s["near"][0]
        seq.done(far)
        s["far"] = over_x(far)

    def swap_near():
        near, far = seq(s["near"], s["far"])
        s["held"] = jnp.concatenate([near, far[None]])
        seq.done(s["held"])
        s["swapped"] = over_core(s["held"])

    def arrived():
        s["swapped"] = seq(s["swapped"])
        seq.done(s["swapped"])

    def pieces():
        return [s[name].reshape(-1, 2, 64, n) for name in ("full", "held", "swapped")]

    parts = [(0, 0), (1, 0), (1, 1), (1, 2), (0, 1), (2, 0), (2, 1), (2, 2)]
    table = [(i, 2 * j + dy) for dy in range(2) for i, j in parts]
    return dict(
        f=products, a1=relay, ac=swap, a2=sum_x, g=gate, b1=spread, b2=spread_x, b3=pass_on, b4=swap_near, d=arrived,
        pieces=pieces, table=table,
    )


def y_first(seq, first, tiles, use):
    s = {}

    def products():
        s["keep"], send = forward("b", first, tiles, seq(use["lhs"]), *use["weights"])
        seq.done(s["keep"])
        s["other"] = over_y(send)

    def sum_y():
        keep, other = seq(s["keep"], s["other"])
        total = keep + other.astype(F32)
        far = total[0].astype(BF16)
        s["near_o"], s["near_k"], s["own"] = total[1].astype(BF16), total[2], total[3]
        seq.done(far)
        s["far"] = over_x(far)

    def relay():
        far, near_k, near_o = seq(s["far"], s["near_k"], s["near_o"])
        near = jnp.stack([(near_k + far.astype(F32)).astype(BF16), near_o])
        seq.done(near)
        s["near"] = over_x(near)

    def swap():
        s["near"] = seq(s["near"])
        other = s["near"][1]
        seq.done(other)
        s["other"] = over_core(other)

    def gate():
        own, near, other = seq(s["own"], s["near"], s["other"])
        use["gated"], s["own"] = gating(first, tiles, [own, near[0], other], use["cot"], use["gated"])
        seq.done(s["own"])
        s["sib"] = over_core(s["own"])

    def spread_x():
        own, s["sib"] = seq(s["own"], s["sib"])
        full = jnp.stack([own, s["sib"]])
        seq.done(full)
        s["near"] = over_x(full)

    def pass_on():
        s["near"] = seq(s["near"])
        far = s["near"][0]
        seq.done(far)
        s["far"] = over_x(far)

    def collect():
        own, near, far = seq(s["own"], s["near"], s["far"])
        s["here"] = jnp.concatenate([own[None], near, far[None]])
        seq.done(s["here"])
        s["there"] = over_y(s["here"])

    def swap_all():
        here, s["there"] = seq(s["here"], s["there"])
        both = jnp.concatenate([here[1:], s["there"]])
        seq.done(both)
        s["swapped"] = over_core(both)

    def arrived():
        s["swapped"] = seq(s["swapped"])
        seq.done(s["swapped"])

    def pieces():
        return [s["here"], s["there"], s["sib"][None], s["swapped"]]

    table = [(0, q) for q in range(4)] + [(2, 0)] + [(3, q) for q in range(3)]
    table += [(1, q) for q in range(4)] + [(3, q) for q in range(3, 7)]
    return dict(
        f=products, b1=sum_y, b2=relay, bc=swap, g=gate, c1=spread_x, c2=pass_on, c3=collect, c4=swap_all, d=arrived,
        pieces=pieces, table=table,
    )


def body(inputs, gate_matrix, lift_matrix, out_cotangent):
    r, c = lax.axis_index("row"), lax.axis_index("col")
    x, yh, k = c // 4, (c // 2) % 2, c % 2

    sib_gate, sib_lift = over_core(gate_matrix), over_core(lift_matrix)
    own_x = lax.all_to_all(jnp.broadcast_to(inputs[None], (8, 128, 512)), "row", 0, 0)
    sib_x = over_core(own_x)

    def block(dx, dy):
        return 2 * ((x + dx) % 4) + (yh + dy) % 2

    fwd = [(2, k), (1 + 2 * k, 1 - k), (1 + 2 * k, k), (0, k)]
    bwd = [(0, k), (3 - 2 * k, k), (3 - 2 * k, 1 - k), (2, k)]
    bwd += [(0, 1 - k), (1 + 2 * k, 1 - k), (1 + 2 * k, k), (2, 1 - k)]
    order = [(block(dx, dy), 64 * h) for dx, h in fwd for dy in range(2)]
    order += [(block(dx, dy), 64 * h) for dy in range(2) for dx, h in bwd]
    at = jnp.stack([jnp.stack([i for i, _ in order]), jnp.stack([h for _, h in order])]).astype(jnp.int32)
    lhs, xt = arrange(at, own_x, sib_x)

    weights = (gate_matrix, sib_gate, lift_matrix, sib_lift)
    use = dict(lhs=lhs, weights=weights, cot=out_cotangent, gated=None)
    seq = Sequence()
    first, steps, spans = 0, [], []
    for path, tiles in CHUNKS:
        steps.append((x_first if path == "a" else y_first)(seq, first, tiles, use))
        spans.append((first, tiles))
        first += tiles

    grads, y, parts = None, None, None
    rest = (xt, gate_matrix, lift_matrix)
    for i, step in ORDER:
        if step[0] != "K":
            steps[i][step]()
            continue
        if step == "Kw":
            pieces = steps[i]["pieces"]()
        else:
            pieces = seq(*steps[i]["pieces"]())
        do = (step != "Ky", step != "Kw")
        grads, y = backward(*spans[i], pieces, steps[i]["table"], *rest, grads, y, *do)
        if step != "Kw":
            seq.done(y)

    def place(i, h):
        row = (r // 4 + i // 4) % 2 * 4 + (r % 4 + i % 4) % 4
        dx, dy = (row // 2 - x) % 4, (row - yh) % 2
        same = (h == k).astype(jnp.int32)
        near = jnp.where(dx == 3 - 2 * k, 2 - same, 5 + same)
        q = jnp.where(dx == 0, 4 - 4 * same, jnp.where(dx == 2, 7 - 4 * same, near))
        return 64 * (8 * dy + q)

    where = jnp.stack([jnp.stack([place(i, h) for h in range(2)]) for i in range(8)]).astype(jnp.int32)
    parts = split(where, y)
    total = parts[0]
    for i in range(1, 8):
        total = total + lax.ppermute(parts[i], "row", row_step(i)).astype(F32)
    return (seq(use["gated"]), total.astype(BF16), grads[0], grads[1])


def solution(mesh):
    return jax.shard_map(
        body,
        mesh=mesh,
        in_specs=(P("row", "col"), P("col", "row"), P("col", "row"), P("col", "row")),
        out_specs=(P("col", "row"), P("row", "col"), P("col", "row"), P("col", "row")),
        check_vma=False,
    )
```

```python
import functools

import jax
import jax.numpy as jnp
from jax import lax
from jax.experimental import pallas as pl
from jax.experimental.pallas import tpu as pltpu
from jax.sharding import PartitionSpec as P

F32, BF16 = jnp.float32, jnp.bfloat16
TILE = 256
CHUNKS = (('b', 3), ('a', 4), ('a', 3), ('a', 3))
ORDER = ((2, 'f'), (3, 'f'), (2, 'a1'), (0, 'f'), (3, 'a1'), (1, 'f'), (2, 'ac'), (0, 'b1'), (3, 'ac'), (2, 'a2'), (1, 'a1'), (3, 'a2'), (2, 'g'), (0, 'b2'), (2, 'b1'), (3, 'g'), (1, 'ac'), (2, 'b2'), (0, 'bc'), (1, 'a2'), (0, 'g'), (0, 'c1'), (1, 'g'), (3, 'b1'), (2, 'b3'), (0, 'c2'), (2, 'b4'), (3, 'b2'), (0, 'c3'), (1, 'b1'), (1, 'b2'), (2, 'd'), (2, 'K'), (3, 'b3'), (0, 'c4'), (1, 'b3'), (3, 'b4'), (0, 'd'), (0, 'K'), (3, 'd'), (1, 'b4'), (3, 'K'), (1, 'd'), (1, 'Ky'), (1, 'Kw'))
MIB = 1 << 20
COST = {'f': 0, 'g': 0.001, 'k': 0.3}


def column(x, y, core):
    return (x % 4) * 4 + (y % 2) * 2 + core % 2


COLS = [(c, c // 4, (c // 2) % 2, c % 2) for c in range(16)]
CORE = [(c, column(x, y, k + 1)) for c, x, y, k in COLS]
ALONG_Y = [(c, column(x, y + 1, k)) for c, x, y, k in COLS]
ALONG_X = [(c, column(x + 1 - 2 * k, y, k)) for c, x, y, k in COLS]


def row_step(i):
    return [(r, ((r // 4 + i // 4) % 2) * 4 + (r % 4 + i % 4) % 4) for r in range(8)]


def over_x(v):
    return lax.ppermute(v, "col", ALONG_X)


def over_y(v):
    return lax.ppermute(v, "col", ALONG_Y)


def over_core(v):
    return lax.ppermute(v, "col", CORE)


def params(mib):
    return pltpu.CompilerParams(vmem_limit_bytes=mib * MIB)


def in_hbm(v):
    return pltpu.with_memory_space_constraint(v, pltpu.HBM)


def whole(shape):
    return pl.BlockSpec(shape, lambda *_: (0,) * len(shape), pipeline_mode=pl.Buffered(1))


SMEM = pl.BlockSpec(memory_space=pltpu.SMEM)
ANY = pl.BlockSpec(memory_space=pl.ANY)


def cost(kind, flops, bytes_accessed):
    part = COST[kind]
    return pl.CostEstimate(flops=int(flops * part), bytes_accessed=int(bytes_accessed * part), transcendentals=0)


def piece(at_ref, ref, i):
    return ref[at_ref[0, i], pl.ds(pl.multiple_of(at_ref[1, i], 64), 64), :]


def arrange_kernel(at_ref, own_ref, sib_ref, lhs_ref):
    for i in range(8):
        lhs_ref[pl.ds(64 * i, 64), :512] = piece(at_ref, own_ref, i)
        lhs_ref[pl.ds(64 * i, 64), 512:] = piece(at_ref, sib_ref, i)


def turn_kernel(at_ref, own_ref, xt_ref):
    for i in range(8):
        pair = [piece(at_ref, own_ref, 8 + 2 * i), piece(at_ref, own_ref, 9 + 2 * i)]
        xt_ref[:, pl.ds(128 * i, 128)] = jnp.concatenate(pair, axis=0).T


def arrange(kernel, at, *blocks):
    return pl.pallas_call(
        kernel,
        out_shape=jax.ShapeDtypeStruct((512, 1024), BF16),
        in_specs=[SMEM] + [whole(v.shape) for v in blocks],
        out_specs=pl.BlockSpec((512, 1024), lambda j: (0, 0)),
        grid=(1,),
        compiler_params=params(8),
        cost_estimate=cost("f", 0, 4 * MIB),
        name="arrange_tokens",
    )(at, *blocks)


def forward_kernel(path, lhs_ref, go_ref, gs_ref, lo_ref, ls_ref, *outs):
    a, b = lhs_ref[:, :512], lhs_ref[:, 512:]
    for m, (o, s) in enumerate(((go_ref, gs_ref), (lo_ref, ls_ref))):
        p = jnp.dot(a, o[...], preferred_element_type=F32)
        p = p + jnp.dot(b, s[...], preferred_element_type=F32)
        for g in range(4):
            for dy in range(2):
                q = p[g * 128 + dy * 64 : g * 128 + dy * 64 + 64]
                if path == "a":
                    outs[g][dy, m] = q.astype(outs[g].dtype)
                else:
                    outs[dy][g, m] = q.astype(outs[dy].dtype)


def forward(path, first, tiles, lhs, own_gate, sib_gate, own_lift, sib_lift):
    n = tiles * TILE
    if path == "a":
        lead, kinds = 2, (BF16, BF16, F32, F32)
    else:
        lead, kinds = 4, (F32, BF16)
    w = pl.BlockSpec((512, TILE), lambda j: (0, first + j))
    return pl.pallas_call(
        functools.partial(forward_kernel, path),
        out_shape=tuple(jax.ShapeDtypeStruct((lead, 2, 64, n), t) for t in kinds),
        in_specs=[whole((512, 1024)), w, w, w, w],
        out_specs=tuple(pl.BlockSpec((lead, 2, 64, TILE), lambda j: (0, 0, 0, j)) for _ in kinds),
        grid=(tiles,),
        compiler_params=params(12),
        cost_estimate=cost("f", 4 * 512 * 1024 * n, 4 * 1024 * n + 6 * 1024 * n),
        name="forward_" + path,
    )(lhs, own_gate, sib_gate, own_lift, sib_lift)


def gate_kernel(terms, *refs):
    total = refs[0][...].astype(F32)
    for ref in refs[1:terms]:
        total = total + ref[...].astype(F32)
    cot = refs[terms][...].astype(F32)
    gated_ref, grads_ref = refs[-2:]
    gate, lift = total[0], total[1]
    sigma = jax.nn.sigmoid(gate)
    silu = gate * sigma
    gated_ref[...] = (silu * lift).astype(BF16)
    grads_ref[0] = (cot * lift * sigma * (1.0 + gate * (1.0 - sigma))).astype(BF16)
    grads_ref[1] = (cot * silu).astype(BF16)


def gating(first, tiles, terms, cot):
    n = tiles * TILE
    return pl.pallas_call(
        functools.partial(gate_kernel, len(terms)),
        out_shape=(jax.ShapeDtypeStruct((64, n), BF16), jax.ShapeDtypeStruct((2, 64, n), BF16)),
        in_specs=[whole((2, 64, n))] * len(terms) + [whole((64, n))],
        out_specs=(pl.BlockSpec((64, n), lambda j: (0, 0)), pl.BlockSpec((2, 64, n), lambda j: (0, 0, 0))),
        grid=(1,),
        compiler_params=params(8),
        cost_estimate=cost("g", 0, 64 * n * 20),
        name="gating",
    )(*terms, cot[:, first * TILE : first * TILE + n])


def tokens(held, table, m):
    return jnp.concatenate([held[i][j, m] for i, j in table], axis=0)


def backward_kernel(arrays, table, with_y, *refs):
    held, (xt_ref, gate_ref, lift_ref) = refs[:arrays], refs[arrays : arrays + 3]
    outs = refs[-3:] if with_y else refs[-2:]
    both = [tokens(held, table, m) for m in range(2)]
    for m in range(2):
        outs[m][...] = jnp.dot(xt_ref[...], both[m], preferred_element_type=F32).astype(BF16)
    if with_y:
        grad = jnp.concatenate(both, axis=1)
        weight = jnp.concatenate([gate_ref[...], lift_ref[...]], axis=1)
        part = lax.dot_general(grad, weight, (((1,), (1,)), ((), ())), preferred_element_type=F32)

        @pl.when(pl.program_id(0) == 0)
        def _():
            outs[2][...] = part

        @pl.when(pl.program_id(0) > 0)
        def _():
            outs[2][...] += part


def backward(first, tiles, pieces, table, xt, gate, lift, grads, with_y):
    n = TILE
    wide = pl.BlockSpec((512, n), lambda j: (0, first + j))
    args = [*pieces, xt, gate, lift]
    specs = [pl.BlockSpec((v.shape[0], 2, 64, n), lambda j: (0, 0, 0, j)) for v in pieces]
    specs += [whole(xt.shape), wide, wide]
    alias, shapes, out_specs = {}, [jax.ShapeDtypeStruct(gate.shape, BF16)] * 2, [wide, wide]
    if with_y:
        shapes.append(jax.ShapeDtypeStruct((1024, 512), F32))
        out_specs.append(pl.BlockSpec((1024, 512), lambda j: (0, 0)))
    if grads is not None:
        for m in range(2):
            alias[len(args)] = m
            args.append(grads[m])
            specs.append(ANY)
    return pl.pallas_call(
        functools.partial(backward_kernel, len(pieces), table, with_y),
        out_shape=tuple(shapes),
        in_specs=specs,
        out_specs=tuple(out_specs),
        grid=(tiles,),
        input_output_aliases=alias,
        compiler_params=params(16),
        cost_estimate=cost("k", (1 + with_y) * 4 * 512 * 1024 * n * tiles, 8 * 1024 * n * tiles + 4 * MIB),
        name="backward",
    )(*args)


def split_kernel(arrays, table, others, at_ref, *refs):
    held, (gate_ref, lift_ref) = refs[:arrays], refs[arrays : arrays + 2]
    y_refs, outs = refs[arrays + 2 : arrays + 2 + others], refs[arrays + 2 + others : -1]
    total_ref = refs[-1]
    grad = jnp.concatenate([tokens(held, table, m) for m in range(2)], axis=1)
    weight = jnp.concatenate([gate_ref[...], lift_ref[...]], axis=1)
    total = lax.dot_general(grad, weight, (((1,), (1,)), ((), ())), preferred_element_type=F32)
    for ref in y_refs:
        total = total + ref[...]
    total_ref[...] = total
    for i in range(8):
        for h in range(2):
            rows = total_ref[pl.ds(pl.multiple_of(at_ref[i, h], 64), 64), :]
            outs[i][pl.ds(64 * h, 64), :] = rows.astype(outs[i].dtype)


def split(at, first, tiles, pieces, table, gate, lift, ys):
    assert first % tiles == 0
    n = tiles * TILE
    kinds = [F32] + [BF16] * 7
    w = pl.BlockSpec((256, n), lambda j: (j, first // tiles))
    return pl.pallas_call(
        functools.partial(split_kernel, len(pieces), table, len(ys)),
        out_shape=tuple(jax.ShapeDtypeStruct((128, 512), t) for t in kinds),
        in_specs=[SMEM]
        + [whole(v.shape) for v in pieces]
        + [w, w]
        + [pl.BlockSpec((1024, 256), lambda j: (0, j))] * len(ys),
        out_specs=tuple(pl.BlockSpec((128, 256), lambda j: (0, j)) for _ in kinds),
        scratch_shapes=[pltpu.VMEM((1024, 256), F32)],
        grid=(2,),
        compiler_params=params(20),
        cost_estimate=cost("k", 4 * 512 * 1024 * n, 8 * 1024 * n + 4 * MIB),
        name="split_rows",
    )(at, *pieces, gate, lift, *ys)


class Sequence:
    def __init__(self):
        self.last = None

    def __call__(self, *values):
        if self.last is not None:
            *values, self.last = lax.optimization_barrier((*values, self.last))
        return values[0] if len(values) == 1 else values

    def done(self, value):
        self.last = value


def x_first(seq, first, tiles, use):
    s = {}
    n = tiles * TILE

    def products():
        s["far"], s["near_o"], s["near_k"], s["own"] = forward("a", first, tiles, seq(use["lhs"]), *use["weights"])
        seq.done(s["near_k"])
        s["far"] = over_x(s["far"])

    def relay():
        far, near_k, near_o = seq(s["far"], s["near_k"], s["near_o"])
        near = jnp.stack([(near_k + far.astype(F32)).astype(BF16), near_o])
        seq.done(near)
        s["near"] = over_x(near)

    def swap():
        s["near"] = seq(s["near"])
        other = s["near"][1]
        seq.done(other)
        s["other"] = over_core(other)

    def sum_x():
        near, other, own = seq(s["near"], s["other"], s["own"])
        total = own + near[0].astype(F32) + other.astype(F32)
        send = total[1].astype(BF16)
        seq.done(send)
        s["own"], s["other"] = total[0], over_y(send)

    def gate():
        own, other = seq(s["own"], s["other"])
        use["gated"][first], s["own"] = gating(first, tiles, [own, other], use["cot"])
        seq.done(s["own"])
        s["other"] = over_y(s["own"])

    def spread():
        own, other = seq(s["own"], s["other"])
        s["own"] = jnp.stack([own, other])
        seq.done(s["own"])
        s["sib"] = over_core(s["own"])

    def spread_x():
        own, sib = seq(s["own"], s["sib"])
        s["full"] = jnp.stack([own, sib])
        seq.done(s["full"])
        s["near"] = over_x(s["full"])

    def pass_on():
        s["near"] = seq(s["near"])
        far = s["near"][0]
        seq.done(far)
        s["far"] = over_x(far)

    def swap_near():
        near, far = seq(s["near"], s["far"])
        s["held"] = jnp.concatenate([near, far[None]])
        seq.done(s["held"])
        s["swapped"] = over_core(s["held"])

    def arrived():
        s["swapped"] = seq(s["swapped"])
        seq.done(s["swapped"])

    def pieces():
        return [s[name].reshape(-1, 2, 64, n) for name in ("full", "held", "swapped")]

    parts = [(0, 0), (1, 0), (1, 1), (1, 2), (0, 1), (2, 0), (2, 1), (2, 2)]
    table = [(i, 2 * j + dy) for dy in range(2) for i, j in parts]
    return dict(
        f=products, a1=relay, ac=swap, a2=sum_x, g=gate, b1=spread, b2=spread_x, b3=pass_on, b4=swap_near, d=arrived,
        pieces=pieces, table=table,
    )


def y_first(seq, first, tiles, use):
    s = {}

    def products():
        s["keep"], send = forward("b", first, tiles, seq(use["lhs"]), *use["weights"])
        seq.done(s["keep"])
        s["other"] = over_y(send)

    def sum_y():
        keep, other = seq(s["keep"], s["other"])
        total = keep + other.astype(F32)
        far = total[0].astype(BF16)
        s["near_o"], s["near_k"], s["own"] = total[1].astype(BF16), total[2], total[3]
        seq.done(far)
        s["far"] = over_x(far)

    def relay():
        far, near_k, near_o = seq(s["far"], s["near_k"], s["near_o"])
        near = jnp.stack([(near_k + far.astype(F32)).astype(BF16), near_o])
        seq.done(near)
        s["near"] = over_x(near)

    def swap():
        s["near"] = seq(s["near"])
        other = s["near"][1]
        seq.done(other)
        s["other"] = over_core(other)

    def gate():
        own, near, other = seq(s["own"], s["near"], s["other"])
        use["gated"][first], s["own"] = gating(first, tiles, [own, near[0], other], use["cot"])
        seq.done(s["own"])
        s["sib"] = over_core(s["own"])

    def spread_x():
        own, s["sib"] = seq(s["own"], s["sib"])
        full = jnp.stack([own, s["sib"]])
        seq.done(full)
        s["near"] = over_x(full)

    def pass_on():
        s["near"] = seq(s["near"])
        far = s["near"][0]
        seq.done(far)
        s["far"] = over_x(far)

    def collect():
        own, near, far = seq(s["own"], s["near"], s["far"])
        s["here"] = jnp.concatenate([own[None], near, far[None]])
        seq.done(s["here"])
        s["there"] = over_y(s["here"])

    def swap_all():
        here, s["there"] = seq(s["here"], s["there"])
        both = jnp.concatenate([here[1:], s["there"]])
        seq.done(both)
        s["swapped"] = over_core(both)

    def arrived():
        s["swapped"] = seq(s["swapped"])
        seq.done(s["swapped"])

    def pieces():
        return [s["here"], s["there"], s["sib"][None], s["swapped"]]

    table = [(0, q) for q in range(4)] + [(2, 0)] + [(3, q) for q in range(3)]
    table += [(1, q) for q in range(4)] + [(3, q) for q in range(3, 7)]
    return dict(
        f=products, b1=sum_y, b2=relay, bc=swap, g=gate, c1=spread_x, c2=pass_on, c3=collect, c4=swap_all, d=arrived,
        pieces=pieces, table=table,
    )


def body(inputs, gate_matrix, lift_matrix, out_cotangent):
    r, c = lax.axis_index("row"), lax.axis_index("col")
    x, yh, k = c // 4, (c // 2) % 2, c % 2

    sib_gate, sib_lift = over_core(gate_matrix), over_core(lift_matrix)
    own_x = lax.all_to_all(jnp.broadcast_to(inputs[None], (8, 128, 512)), "row", 0, 0)
    sib_x = over_core(own_x)

    def block(dx, dy):
        return 2 * ((x + dx) % 4) + (yh + dy) % 2

    fwd = [(2, k), (1 + 2 * k, 1 - k), (1 + 2 * k, k), (0, k)]
    bwd = [(0, k), (3 - 2 * k, k), (3 - 2 * k, 1 - k), (2, k)]
    bwd += [(0, 1 - k), (1 + 2 * k, 1 - k), (1 + 2 * k, k), (2, 1 - k)]
    order = [(block(dx, dy), 64 * h) for dx, h in fwd for dy in range(2)]
    order += [(block(dx, dy), 64 * h) for dy in range(2) for dx, h in bwd]
    at = jnp.stack([jnp.stack([i for i, _ in order]), jnp.stack([h for _, h in order])]).astype(jnp.int32)
    def place(i, h):
        row = (r // 4 + i // 4) % 2 * 4 + (r % 4 + i % 4) % 4
        dx, dy = (row // 2 - x) % 4, (row - yh) % 2
        same = (h == k).astype(jnp.int32)
        near = jnp.where(dx == 3 - 2 * k, 2 - same, 5 + same)
        q = jnp.where(dx == 0, 4 - 4 * same, jnp.where(dx == 2, 7 - 4 * same, near))
        return 64 * (8 * dy + q)

    where = jnp.stack([jnp.stack([place(i, h) for h in range(2)]) for i in range(8)]).astype(jnp.int32)
    at, where = lax.optimization_barrier((at, where))
    lhs = arrange(arrange_kernel, at, own_x, sib_x)

    own_gate, own_lift = in_hbm(gate_matrix), in_hbm(lift_matrix)
    weights = (own_gate, sib_gate, own_lift, sib_lift)
    use = dict(lhs=lhs, weights=weights, cot=out_cotangent, gated={})
    seq = Sequence()
    steps, spans, last = [], [], ORDER[-1][0]
    for i, (path, tiles) in enumerate(CHUNKS):
        first = sum(t for j, (_, t) in enumerate(CHUNKS) if (j != last, t, j) < (i != last, tiles, i))
        steps.append((x_first if path == "a" else y_first)(seq, first, tiles, use))
        spans.append((first, tiles))

    grads, ys, xt = None, [], None
    for i, step in ORDER:
        if step == "a2" and xt is None:
            xt = arrange(turn_kernel, at, seq(own_x))
            seq.done(xt)
        if step[0] != "K":
            steps[i][step]()
            continue
        pieces = seq(*steps[i]["pieces"]())
        table = steps[i]["table"]
        if step == "Ky":
            assert len(ys) == len(CHUNKS) - 1
            parts = split(where, *spans[i], pieces, table, own_gate, own_lift, ys)
            got = {i: lax.ppermute(parts[i], "row", row_step(i)) for i in (6, 2, 5, 7, 1, 3, 4)}
            got[6], got[2] = seq(got[6], got[2])
            seq.done(got[2])
            continue
        grads = backward(*spans[i], pieces, table, xt, own_gate, own_lift, grads, step == "K")
        if step == "K":
            seq.done(grads[2])
            ys.append(grads[2])

    total = parts[0]
    for i in range(1, 8):
        total = total + got[i].astype(F32)
    gated = jnp.concatenate([use["gated"][first] for first in sorted(use["gated"])], axis=1)
    return (gated, total.astype(BF16), grads[0], grads[1])


def solution(mesh):
    return jax.shard_map(
        body,
        mesh=mesh,
        in_specs=(P("row", "col"), P("col", "row"), P("col", "row"), P("col", "row")),
        out_specs=(P("col", "row"), P("row", "col"), P("col", "row"), P("col", "row")),
        check_vma=False,
    )
```

```python
import functools

import jax
import jax.numpy as jnp
from jax import lax
from jax.experimental import pallas as pl
from jax.experimental.pallas import tpu as pltpu
from jax.sharding import PartitionSpec as P

F32, BF16 = jnp.float32, jnp.bfloat16
TILE = 256
CHUNKS = (('b', 3), ('a', 4), ('a', 3), ('a', 3))
ORDER = ((2, 'f'), (3, 'f'), (0, 'f'), (2, 'a1'), (3, 'a1'), (1, 'f'), (0, 'b1'), (2, 'ac'), (3, 'ac'), (2, 'a2'), (1, 'a1'), (3, 'a2'), (2, 'g'), (0, 'b2'), (2, 'b1'), (3, 'g'), (1, 'ac'), (2, 'b2'), (0, 'bc'), (1, 'a2'), (0, 'g'), (0, 'c1'), (1, 'g'), (3, 'b1'), (2, 'b3'), (0, 'c2'), (2, 'b4'), (3, 'b2'), (0, 'c3'), (1, 'b1'), (1, 'b2'), (2, 'd'), (2, 'K'), (3, 'b3'), (0, 'c4'), (1, 'b3'), (3, 'b4'), (0, 'd'), (0, 'K'), (3, 'd'), (1, 'b4'), (3, 'K'), (1, 'd'), (1, 'Ky'), (1, 'Kw'))
MIB = 1 << 20
APART = ()
COST = {'f': 0, 'g': 0.001, 'k': 0.001}


def column(x, y, core):
    return (x % 4) * 4 + (y % 2) * 2 + core % 2


COLS = [(c, c // 4, (c // 2) % 2, c % 2) for c in range(16)]
CORE = [(c, column(x, y, k + 1)) for c, x, y, k in COLS]
ALONG_Y = [(c, column(x, y + 1, k)) for c, x, y, k in COLS]
ALONG_X = [(c, column(x + 1 - 2 * k, y, k)) for c, x, y, k in COLS]


def row_step(i):
    return [(r, ((r // 4 + i // 4) % 2) * 4 + (r % 4 + i % 4) % 4) for r in range(8)]


def over_x(v):
    return lax.ppermute(v, "col", ALONG_X)


def over_y(v):
    return lax.ppermute(v, "col", ALONG_Y)


def over_core(v):
    return lax.ppermute(v, "col", CORE)


def params(mib):
    return pltpu.CompilerParams(vmem_limit_bytes=mib * MIB)


def in_hbm(v):
    return pltpu.with_memory_space_constraint(v, pltpu.HBM)


def whole(shape):
    return pl.BlockSpec(shape, lambda *_: (0,) * len(shape), pipeline_mode=pl.Buffered(1))


SMEM = pl.BlockSpec(memory_space=pltpu.SMEM)
ANY = pl.BlockSpec(memory_space=pl.ANY)


def cost(kind, flops, bytes_accessed):
    part = COST[kind]
    return pl.CostEstimate(flops=int(flops * part), bytes_accessed=int(bytes_accessed * part), transcendentals=0)


def piece(at_ref, ref, i):
    return ref[at_ref[0, i], pl.ds(pl.multiple_of(at_ref[1, i], 64), 64), :]


def arrange_kernel(at_ref, own_ref, sib_ref, lhs_ref):
    for i in range(8):
        lhs_ref[pl.ds(64 * i, 64), :512] = piece(at_ref, own_ref, i)
        lhs_ref[pl.ds(64 * i, 64), 512:] = piece(at_ref, sib_ref, i)


def turn_kernel(at_ref, own_ref, xt_ref):
    for i in range(8):
        pair = [piece(at_ref, own_ref, 8 + 2 * i), piece(at_ref, own_ref, 9 + 2 * i)]
        xt_ref[:, pl.ds(128 * i, 128)] = jnp.concatenate(pair, axis=0).T


def arrange(kernel, at, *blocks):
    return pl.pallas_call(
        kernel,
        out_shape=jax.ShapeDtypeStruct((512, 1024), BF16),
        in_specs=[SMEM] + [whole(v.shape) for v in blocks],
        out_specs=pl.BlockSpec((512, 1024), lambda j: (0, 0)),
        grid=(1,),
        compiler_params=params(8),
        cost_estimate=cost("f", 0, 4 * MIB),
        name="arrange_tokens",
    )(at, *blocks)


def forward_kernel(path, lhs_ref, go_ref, gs_ref, lo_ref, ls_ref, *outs):
    a, b = lhs_ref[:, :512], lhs_ref[:, 512:]
    for m, (o, s) in enumerate(((go_ref, gs_ref), (lo_ref, ls_ref))):
        p = jnp.dot(a, o[...], preferred_element_type=F32)
        p = p + jnp.dot(b, s[...], preferred_element_type=F32)
        for g in range(4):
            for dy in range(2):
                q = p[g * 128 + dy * 64 : g * 128 + dy * 64 + 64]
                if path == "a":
                    outs[g][dy, m] = q.astype(outs[g].dtype)
                else:
                    outs[dy][g, m] = q.astype(outs[dy].dtype)


def forward(path, first, tiles, lhs, own_gate, sib_gate, own_lift, sib_lift):
    n = tiles * TILE
    if path == "a":
        lead, kinds = 2, (BF16, BF16, F32, F32)
    else:
        lead, kinds = 4, (F32, BF16)
    w = pl.BlockSpec((512, TILE), lambda j: (0, first + j))
    return pl.pallas_call(
        functools.partial(forward_kernel, path),
        out_shape=tuple(jax.ShapeDtypeStruct((lead, 2, 64, n), t) for t in kinds),
        in_specs=[whole((512, 1024)), w, w, w, w],
        out_specs=tuple(pl.BlockSpec((lead, 2, 64, TILE), lambda j: (0, 0, 0, j)) for _ in kinds),
        grid=(tiles,),
        compiler_params=params(12),
        cost_estimate=cost("f", 4 * 512 * 1024 * n, 4 * 1024 * n + 6 * 1024 * n),
        name="forward_" + path,
    )(lhs, own_gate, sib_gate, own_lift, sib_lift)


def gate_kernel(terms, *refs):
    total = refs[0][...].astype(F32)
    for ref in refs[1:terms]:
        total = total + ref[...].astype(F32)
    cot = refs[terms][...].astype(F32)
    gated_ref, grads_ref = refs[-2:]
    gate, lift = total[0], total[1]
    sigma = jax.nn.sigmoid(gate)
    silu = gate * sigma
    gated_ref[...] = (silu * lift).astype(BF16)
    grads_ref[0] = (cot * lift * sigma * (1.0 + gate * (1.0 - sigma))).astype(BF16)
    grads_ref[1] = (cot * silu).astype(BF16)


def gating(first, tiles, terms, cot):
    n = tiles * TILE
    return pl.pallas_call(
        functools.partial(gate_kernel, len(terms)),
        out_shape=(jax.ShapeDtypeStruct((64, n), BF16), jax.ShapeDtypeStruct((2, 64, n), BF16)),
        in_specs=[whole((2, 64, n))] * len(terms) + [whole((64, n))],
        out_specs=(pl.BlockSpec((64, n), lambda j: (0, 0)), pl.BlockSpec((2, 64, n), lambda j: (0, 0, 0))),
        grid=(1,),
        compiler_params=params(8),
        cost_estimate=cost("g", 0, 64 * n * 20),
        name="gating",
    )(*terms, cot[:, first * TILE : first * TILE + n])


def tokens(held, table, m):
    return jnp.concatenate([held[i][j, m] for i, j in table], axis=0)


def backward_kernel(arrays, table, with_y, *refs):
    held, (xt_ref, gate_ref, lift_ref) = refs[:arrays], refs[arrays : arrays + 3]
    outs = refs[-3:] if with_y else refs[-2:]
    both = [tokens(held, table, m) for m in range(2)]
    for m in range(2):
        outs[m][...] = jnp.dot(xt_ref[...], both[m], preferred_element_type=F32).astype(BF16)
    if with_y:
        grad = jnp.concatenate(both, axis=1)
        weight = jnp.concatenate([gate_ref[...], lift_ref[...]], axis=1)
        part = lax.dot_general(grad, weight, (((1,), (1,)), ((), ())), preferred_element_type=F32)

        @pl.when(pl.program_id(0) == 0)
        def _():
            outs[2][...] = part

        @pl.when(pl.program_id(0) > 0)
        def _():
            outs[2][...] += part


def backward(first, tiles, pieces, table, xt, gate, lift, grads, with_y):
    once = first % tiles == 0
    n = tiles * TILE if once else TILE
    mode = dict(pipeline_mode=pl.Buffered(1)) if once else {}
    wide = pl.BlockSpec((512, n), lambda j: (0, first // tiles if once else first + j), **mode)
    args = [*pieces, xt, gate, lift]
    specs = [pl.BlockSpec((v.shape[0], 2, 64, n), lambda j: (0, 0, 0, j), **mode) for v in pieces]
    specs += [whole(xt.shape), wide, wide]
    alias, shapes = {}, [jax.ShapeDtypeStruct(gate.shape, BF16)] * 2
    column = pl.BlockSpec((512, n), lambda j: (0, first // tiles if once else first + j))
    out_specs = [column, column]
    if with_y:
        shapes.append(jax.ShapeDtypeStruct((1024, 512), F32))
        out_specs.append(pl.BlockSpec((1024, 512), lambda j: (0, 0)))
    if grads is not None:
        for m in range(2):
            alias[len(args)] = m
            args.append(grads[m])
            specs.append(ANY)
    return pl.pallas_call(
        functools.partial(backward_kernel, len(pieces), table, with_y),
        out_shape=tuple(shapes),
        in_specs=specs,
        out_specs=tuple(out_specs),
        grid=(1 if once else tiles,),
        input_output_aliases=alias,
        compiler_params=params(28 if once else 16),
        cost_estimate=cost("k", (1 + with_y) * 4 * 512 * 1024 * n * tiles, 8 * 1024 * n * tiles + 4 * MIB),
        name="backward",
    )(*args)


def split_kernel(arrays, table, tiles, others, at_ref, *refs):
    held, w_refs = refs[:arrays], refs[arrays : arrays + 2 * tiles]
    y_refs, outs = refs[arrays + 2 * tiles :][:others], refs[arrays + 2 * tiles + others : -1]
    total_ref = refs[-1]
    grad = jnp.concatenate([tokens(held, table, m) for m in range(2)], axis=1)
    weight = jnp.concatenate([ref[...] for ref in w_refs], axis=1)
    total = lax.dot_general(grad, weight, (((1,), (1,)), ((), ())), preferred_element_type=F32)
    for ref in y_refs:
        total = total + ref[...]
    total_ref[...] = total
    for i in range(8):
        for h in range(2):
            rows = total_ref[pl.ds(pl.multiple_of(at_ref[i, h], 64), 64), :]
            outs[i][pl.ds(64 * h, 64), :] = rows.astype(outs[i].dtype)


def split(at, first, tiles, pieces, table, gate, lift, ys):
    n = tiles * TILE
    kinds = [F32] + [BF16] * 7
    w = [pl.BlockSpec((256, TILE), lambda j, t=t: (j, first + t)) for t in range(tiles)]
    return pl.pallas_call(
        functools.partial(split_kernel, len(pieces), table, tiles, len(ys)),
        out_shape=tuple(jax.ShapeDtypeStruct((128, 512), t) for t in kinds),
        in_specs=[SMEM]
        + [whole(v.shape) for v in pieces]
        + w
        + w
        + [pl.BlockSpec((1024, 256), lambda j: (0, j))] * len(ys),
        out_specs=tuple(pl.BlockSpec((128, 256), lambda j: (0, j)) for _ in kinds),
        scratch_shapes=[pltpu.VMEM((1024, 256), F32)],
        grid=(2,),
        compiler_params=params(24),
        cost_estimate=cost("k", 4 * 512 * 1024 * n, 8 * 1024 * n + 4 * MIB),
        name="split_rows",
    )(at, *pieces, *[gate] * tiles, *[lift] * tiles, *ys)


class Sequence:
    def __init__(self):
        self.last = None

    def __call__(self, *values):
        if self.last is not None:
            *values, self.last = lax.optimization_barrier((*values, self.last))
        return values[0] if len(values) == 1 else values

    def done(self, value):
        self.last = value


def x_first(seq, first, tiles, use, apart):
    s = {}
    n = tiles * TILE

    def products():
        s["far"], s["near_o"], s["near_k"], s["own"] = forward("a", first, tiles, seq(use["lhs"]), *use["weights"])
        seq.done(s["near_k"])
        s["far"] = over_x(s["far"])

    def relay():
        far, near_k, near_o = seq(s["far"], s["near_k"], s["near_o"])
        near = jnp.stack([(near_k + far.astype(F32)).astype(BF16), near_o])
        seq.done(near)
        s["near"] = over_x(near)

    def swap():
        s["near"] = seq(s["near"])
        other = s["near"][1]
        seq.done(other)
        s["other"] = over_core(other)

    def sum_x():
        near, other, own = seq(s["near"], s["other"], s["own"])
        total = own + near[0].astype(F32) + other.astype(F32)
        send = total[1].astype(BF16)
        seq.done(send)
        s["own"], s["other"] = total[0], over_y(send)

    def gate():
        own, other = seq(s["own"], s["other"])
        use["gated"][first], s["own"] = gating(first, tiles, [own, other], use["cot"])
        seq.done(s["own"])
        s["other"] = over_y(s["own"])

    def spread():
        own, other = seq(s["own"], s["other"])
        s["own"] = jnp.stack([own, other])
        seq.done(s["own"])
        if apart:
            s["near_k"] = over_x(s["own"])
        s["sib"] = over_core(s["own"])

    def spread_x():
        own, sib = seq(s["own"], s["sib"])
        s["full"] = jnp.stack([own, sib])
        seq.done(s["full"])
        if apart:
            s["near_o"] = over_x(sib)
        else:
            s["near"] = over_x(s["full"])

    def pass_on():
        if apart:
            far = s["near_k"] = seq(s["near_k"])
        else:
            s["near"] = seq(s["near"])
            far = s["near"][0]
        seq.done(far)
        s["far"] = over_x(far)

    def swap_near():
        if apart:
            s["held"] = jnp.stack(seq(s["near_k"], s["near_o"], s["far"]))
        else:
            near, far = seq(s["near"], s["far"])
            s["held"] = jnp.concatenate([near, far[None]])
        seq.done(s["held"])
        s["swapped"] = over_core(s["held"])

    def arrived():
        s["swapped"] = seq(s["swapped"])
        seq.done(s["swapped"])

    def pieces():
        return [s[name].reshape(-1, 2, 64, n) for name in ("full", "held", "swapped")]

    parts = [(0, 0), (1, 0), (1, 1), (1, 2), (0, 1), (2, 0), (2, 1), (2, 2)]
    table = [(i, 2 * j + dy) for dy in range(2) for i, j in parts]
    return dict(
        f=products, a1=relay, ac=swap, a2=sum_x, g=gate, b1=spread, b2=spread_x, b3=pass_on, b4=swap_near, d=arrived,
        pieces=pieces, table=table,
    )


def y_first(seq, first, tiles, use, apart):
    s = {}

    def products():
        s["keep"], send = forward("b", first, tiles, seq(use["lhs"]), *use["weights"])
        seq.done(s["keep"])
        s["other"] = over_y(send)

    def sum_y():
        keep, other = seq(s["keep"], s["other"])
        total = keep + other.astype(F32)
        far = total[0].astype(BF16)
        s["near_o"], s["near_k"], s["own"] = total[1].astype(BF16), total[2], total[3]
        seq.done(far)
        s["far"] = over_x(far)

    def relay():
        far, near_k, near_o = seq(s["far"], s["near_k"], s["near_o"])
        near = jnp.stack([(near_k + far.astype(F32)).astype(BF16), near_o])
        seq.done(near)
        s["near"] = over_x(near)

    def swap():
        s["near"] = seq(s["near"])
        other = s["near"][1]
        seq.done(other)
        s["other"] = over_core(other)

    def gate():
        own, near, other = seq(s["own"], s["near"], s["other"])
        use["gated"][first], s["own"] = gating(first, tiles, [own, near[0], other], use["cot"])
        seq.done(s["own"])
        if apart:
            s["near_k"] = over_x(s["own"])
        s["sib"] = over_core(s["own"])

    def spread_x():
        own, s["sib"] = seq(s["own"], s["sib"])
        if apart:
            seq.done(s["sib"])
            s["near_o"] = over_x(s["sib"])
        else:
            full = jnp.stack([own, s["sib"]])
            seq.done(full)
            s["near"] = over_x(full)

    def pass_on():
        if apart:
            far = s["near_k"] = seq(s["near_k"])
        else:
            s["near"] = seq(s["near"])
            far = s["near"][0]
        seq.done(far)
        s["far"] = over_x(far)

    def collect():
        if apart:
            s["here"] = jnp.stack(seq(s["own"], s["near_k"], s["near_o"], s["far"]))
        else:
            own, near, far = seq(s["own"], s["near"], s["far"])
            s["here"] = jnp.concatenate([own[None], near, far[None]])
        seq.done(s["here"])
        s["there"] = over_y(s["here"])

    def swap_all():
        here, s["there"] = seq(s["here"], s["there"])
        both = jnp.concatenate([here[1:], s["there"]])
        seq.done(both)
        s["swapped"] = over_core(both)

    def arrived():
        s["swapped"] = seq(s["swapped"])
        seq.done(s["swapped"])

    def pieces():
        return [s["here"], s["there"], s["sib"][None], s["swapped"]]

    table = [(0, q) for q in range(4)] + [(2, 0)] + [(3, q) for q in range(3)]
    table += [(1, q) for q in range(4)] + [(3, q) for q in range(3, 7)]
    return dict(
        f=products, b1=sum_y, b2=relay, bc=swap, g=gate, c1=spread_x, c2=pass_on, c3=collect, c4=swap_all, d=arrived,
        pieces=pieces, table=table,
    )


def body(inputs, gate_matrix, lift_matrix, out_cotangent):
    r, c = lax.axis_index("row"), lax.axis_index("col")
    x, yh, k = c // 4, (c // 2) % 2, c % 2

    sib_gate, sib_lift = over_core(gate_matrix), over_core(lift_matrix)
    own_x = lax.all_to_all(jnp.broadcast_to(inputs[None], (8, 128, 512)), "row", 0, 0)
    sib_x = over_core(own_x)

    def block(dx, dy):
        return 2 * ((x + dx) % 4) + (yh + dy) % 2

    fwd = [(2, k), (1 + 2 * k, 1 - k), (1 + 2 * k, k), (0, k)]
    bwd = [(0, k), (3 - 2 * k, k), (3 - 2 * k, 1 - k), (2, k)]
    bwd += [(0, 1 - k), (1 + 2 * k, 1 - k), (1 + 2 * k, k), (2, 1 - k)]
    order = [(block(dx, dy), 64 * h) for dx, h in fwd for dy in range(2)]
    order += [(block(dx, dy), 64 * h) for dy in range(2) for dx, h in bwd]
    at = jnp.stack([jnp.stack([i for i, _ in order]), jnp.stack([h for _, h in order])]).astype(jnp.int32)
    def place(i, h):
        row = (r // 4 + i // 4) % 2 * 4 + (r % 4 + i % 4) % 4
        dx, dy = (row // 2 - x) % 4, (row - yh) % 2
        same = (h == k).astype(jnp.int32)
        near = jnp.where(dx == 3 - 2 * k, 2 - same, 5 + same)
        q = jnp.where(dx == 0, 4 - 4 * same, jnp.where(dx == 2, 7 - 4 * same, near))
        return 64 * (8 * dy + q)

    where = jnp.stack([jnp.stack([place(i, h) for h in range(2)]) for i in range(8)]).astype(jnp.int32)
    at, where = lax.optimization_barrier((at, where))
    lhs = arrange(arrange_kernel, at, own_x, sib_x)

    own_gate, own_lift = in_hbm(gate_matrix), in_hbm(lift_matrix)
    weights = (own_gate, sib_gate, own_lift, sib_lift)
    use = dict(lhs=lhs, weights=weights, cot=out_cotangent, gated={})
    seq = Sequence()
    steps, spans = [], []
    for i, (path, tiles) in enumerate(CHUNKS):
        first = sum(t for j, (_, t) in enumerate(CHUNKS) if (t, j) < (tiles, i))
        steps.append((x_first if path == "a" else y_first)(seq, first, tiles, use, i in APART))
        spans.append((first, tiles))

    grads, ys, xt = None, [], None
    for i, step in ORDER:
        if step == "a2" and xt is None:
            xt = arrange(turn_kernel, at, seq(own_x))
            seq.done(xt)
        if step[0] != "K":
            steps[i][step]()
            if step == "g" and len(use["gated"]) == len(CHUNKS):
                gated = jnp.concatenate([use["gated"][first] for first in sorted(use["gated"])], axis=1)
                seq.done(gated)
            continue
        pieces = seq(*steps[i]["pieces"]())
        table = steps[i]["table"]
        if step == "Ky":
            assert len(ys) == len(CHUNKS) - 1
            parts = split(where, *spans[i], pieces, table, own_gate, own_lift, ys)
            got = {i: lax.ppermute(parts[i], "row", row_step(i)) for i in (6, 2, 5, 7, 1, 3, 4)}
            got[6], got[2] = seq(got[6], got[2])
            seq.done(got[2])
            continue
        grads = backward(*spans[i], pieces, table, xt, own_gate, own_lift, grads, step == "K")
        if step == "K":
            seq.done(grads[2])
            ys.append(grads[2])

    total = parts[0]
    for i in range(1, 8):
        total = total + got[i].astype(F32)
    return (gated, total.astype(BF16), grads[0], grads[1])


def solution(mesh):
    return jax.shard_map(
        body,
        mesh=mesh,
        in_specs=(P("row", "col"), P("col", "row"), P("col", "row"), P("col", "row")),
        out_specs=(P("col", "row"), P("row", "col"), P("col", "row"), P("col", "row")),
        check_vma=False,
    )
```

```python
import functools

import jax
import jax.numpy as jnp
from jax import lax
from jax.experimental import pallas as pl
from jax.experimental.pallas import tpu as pltpu
from jax.sharding import PartitionSpec as P

F32, BF16 = jnp.float32, jnp.bfloat16
TILE = 256
CHUNKS = (('b', 3), ('a', 4), ('a', 3), ('a', 3))
ORDER = ((2, 'f'), (3, 'f'), (2, 'a1'), (0, 'f'), (3, 'a1'), (1, 'f'), (2, 'ac'), (0, 'b1'), (3, 'ac'), (2, 'a2'), (1, 'a1'), (3, 'a2'), (2, 'g'), (0, 'b2'), (2, 'b1'), (3, 'g'), (1, 'ac'), (2, 'b2'), (0, 'bc'), (1, 'a2'), (0, 'g'), (0, 'c1'), (1, 'g'), (3, 'b1'), (2, 'b3'), (0, 'c2'), (2, 'b4'), (3, 'b2'), (0, 'c3'), (1, 'b1'), (1, 'b2'), (2, 'd'), (2, 'K'), (3, 'b3'), (0, 'c4'), (1, 'b3'), (3, 'b4'), (0, 'd'), (0, 'K'), (3, 'd'), (1, 'b4'), (3, 'K'), (1, 'd'), (1, 'Ky'), (1, 'Kw'))
MIB = 1 << 20
APART = ()
COST = {'f': 0, 'g': 0.001, 'k': 0.3}


def column(x, y, core):
    return (x % 4) * 4 + (y % 2) * 2 + core % 2


COLS = [(c, c // 4, (c // 2) % 2, c % 2) for c in range(16)]
CORE = [(c, column(x, y, k + 1)) for c, x, y, k in COLS]
ALONG_Y = [(c, column(x, y + 1, k)) for c, x, y, k in COLS]
ALONG_X = [(c, column(x + 1 - 2 * k, y, k)) for c, x, y, k in COLS]


def row_step(i):
    return [(r, ((r // 4 + i // 4) % 2) * 4 + (r % 4 + i % 4) % 4) for r in range(8)]


def over_x(v):
    return lax.ppermute(v, "col", ALONG_X)


def over_y(v):
    return lax.ppermute(v, "col", ALONG_Y)


def over_core(v):
    return lax.ppermute(v, "col", CORE)


def params(mib):
    return pltpu.CompilerParams(vmem_limit_bytes=mib * MIB)


def in_hbm(v):
    return pltpu.with_memory_space_constraint(v, pltpu.HBM)


def whole(shape):
    return pl.BlockSpec(shape, lambda *_: (0,) * len(shape), pipeline_mode=pl.Buffered(1))


SMEM = pl.BlockSpec(memory_space=pltpu.SMEM)
ANY = pl.BlockSpec(memory_space=pl.ANY)


def cost(kind, flops, bytes_accessed):
    part = COST[kind]
    return pl.CostEstimate(flops=int(flops * part), bytes_accessed=int(bytes_accessed * part), transcendentals=0)


def piece(at_ref, ref, i):
    return ref[at_ref[0, i], pl.ds(pl.multiple_of(at_ref[1, i], 64), 64), :]


def arrange_kernel(at_ref, own_ref, sib_ref, lhs_ref):
    for i in range(8):
        lhs_ref[pl.ds(64 * i, 64), :512] = piece(at_ref, own_ref, i)
        lhs_ref[pl.ds(64 * i, 64), 512:] = piece(at_ref, sib_ref, i)


def turn_kernel(at_ref, own_ref, xt_ref):
    for i in range(8):
        pair = [piece(at_ref, own_ref, 8 + 2 * i), piece(at_ref, own_ref, 9 + 2 * i)]
        xt_ref[:, pl.ds(128 * i, 128)] = jnp.concatenate(pair, axis=0).T


def arrange(kernel, at, *blocks):
    return pl.pallas_call(
        kernel,
        out_shape=jax.ShapeDtypeStruct((512, 1024), BF16),
        in_specs=[SMEM] + [whole(v.shape) for v in blocks],
        out_specs=pl.BlockSpec((512, 1024), lambda j: (0, 0)),
        grid=(1,),
        compiler_params=params(8),
        cost_estimate=cost("f", 0, 4 * MIB),
        name="arrange_tokens",
    )(at, *blocks)


def forward_kernel(path, lhs_ref, go_ref, gs_ref, lo_ref, ls_ref, *outs):
    a, b = lhs_ref[:, :512], lhs_ref[:, 512:]
    for m, (o, s) in enumerate(((go_ref, gs_ref), (lo_ref, ls_ref))):
        p = jnp.dot(a, o[...], preferred_element_type=F32)
        p = p + jnp.dot(b, s[...], preferred_element_type=F32)
        for g in range(4):
            for dy in range(2):
                q = p[g * 128 + dy * 64 : g * 128 + dy * 64 + 64]
                if path == "a":
                    outs[g][dy, m] = q.astype(outs[g].dtype)
                else:
                    outs[dy][g, m] = q.astype(outs[dy].dtype)


def forward(path, first, tiles, lhs, own_gate, sib_gate, own_lift, sib_lift):
    n = tiles * TILE
    if path == "a":
        lead, kinds = 2, (BF16, BF16, F32, F32)
    else:
        lead, kinds = 4, (F32, BF16)
    w = pl.BlockSpec((512, TILE), lambda j: (0, first + j))
    return pl.pallas_call(
        functools.partial(forward_kernel, path),
        out_shape=tuple(jax.ShapeDtypeStruct((lead, 2, 64, n), t) for t in kinds),
        in_specs=[whole((512, 1024)), w, w, w, w],
        out_specs=tuple(pl.BlockSpec((lead, 2, 64, TILE), lambda j: (0, 0, 0, j)) for _ in kinds),
        grid=(tiles,),
        compiler_params=params(12),
        cost_estimate=cost("f", 4 * 512 * 1024 * n, 4 * 1024 * n + 6 * 1024 * n),
        name="forward_" + path,
    )(lhs, own_gate, sib_gate, own_lift, sib_lift)


def gate_kernel(terms, *refs):
    total = refs[0][...].astype(F32)
    for ref in refs[1:terms]:
        total = total + ref[...].astype(F32)
    cot = refs[terms][...].astype(F32)
    gated_ref, grads_ref = refs[-2:]
    gate, lift = total[0], total[1]
    sigma = jax.nn.sigmoid(gate)
    silu = gate * sigma
    gated_ref[...] = (silu * lift).astype(BF16)
    grads_ref[0] = (cot * lift * sigma * (1.0 + gate * (1.0 - sigma))).astype(BF16)
    grads_ref[1] = (cot * silu).astype(BF16)


def gating(first, tiles, terms, cot):
    n = tiles * TILE
    return pl.pallas_call(
        functools.partial(gate_kernel, len(terms)),
        out_shape=(jax.ShapeDtypeStruct((64, n), BF16), jax.ShapeDtypeStruct((2, 64, n), BF16)),
        in_specs=[whole((2, 64, n))] * len(terms) + [whole((64, n))],
        out_specs=(pl.BlockSpec((64, n), lambda j: (0, 0)), pl.BlockSpec((2, 64, n), lambda j: (0, 0, 0))),
        grid=(1,),
        compiler_params=params(8),
        cost_estimate=cost("g", 0, 64 * n * 20),
        name="gating",
    )(*terms, cot[:, first * TILE : first * TILE + n])


def tokens(held, table, m):
    return jnp.concatenate([held[i][j, m] for i, j in table], axis=0)


def backward_kernel(arrays, table, with_y, *refs):
    held, (xt_ref, gate_ref, lift_ref) = refs[:arrays], refs[arrays : arrays + 3]
    outs = refs[-3:] if with_y else refs[-2:]
    both = [tokens(held, table, m) for m in range(2)]
    for m in range(2):
        outs[m][...] = jnp.dot(xt_ref[...], both[m], preferred_element_type=F32).astype(BF16)
    if with_y:
        grad = jnp.concatenate(both, axis=1)
        weight = jnp.concatenate([gate_ref[...], lift_ref[...]], axis=1)
        part = lax.dot_general(grad, weight, (((1,), (1,)), ((), ())), preferred_element_type=F32)

        @pl.when(pl.program_id(0) == 0)
        def _():
            outs[2][...] = part

        @pl.when(pl.program_id(0) > 0)
        def _():
            outs[2][...] += part


def backward(first, tiles, pieces, table, xt, gate, lift, grads, with_y):
    once = first % tiles == 0
    n = tiles * TILE if once else TILE
    mode = dict(pipeline_mode=pl.Buffered(1)) if once else {}
    wide = pl.BlockSpec((512, n), lambda j: (0, first // tiles if once else first + j), **mode)
    args = [*pieces, xt, gate, lift]
    specs = [pl.BlockSpec((v.shape[0], 2, 64, n), lambda j: (0, 0, 0, j), **mode) for v in pieces]
    specs += [whole(xt.shape), wide, wide]
    alias, shapes = {}, [jax.ShapeDtypeStruct(gate.shape, BF16)] * 2
    column = pl.BlockSpec((512, n), lambda j: (0, first // tiles if once else first + j))
    out_specs = [column, column]
    if with_y:
        shapes.append(jax.ShapeDtypeStruct((1024, 512), F32))
        out_specs.append(pl.BlockSpec((1024, 512), lambda j: (0, 0)))
    if grads is not None:
        for m in range(2):
            alias[len(args)] = m
            args.append(grads[m])
            specs.append(ANY)
    return pl.pallas_call(
        functools.partial(backward_kernel, len(pieces), table, with_y),
        out_shape=tuple(shapes),
        in_specs=specs,
        out_specs=tuple(out_specs),
        grid=(1 if once else tiles,),
        input_output_aliases=alias,
        compiler_params=params(28 if once else 16),
        cost_estimate=cost("k", (1 + with_y) * 4 * 512 * 1024 * n * tiles, 8 * 1024 * n * tiles + 4 * MIB),
        name="backward",
    )(*args)


def split_kernel(arrays, table, tiles, others, at_ref, *refs):
    held, w_refs = refs[:arrays], refs[arrays : arrays + 2 * tiles]
    y_refs, outs = refs[arrays + 2 * tiles :][:others], refs[arrays + 2 * tiles + others : -1]
    total_ref = refs[-1]
    grad = jnp.concatenate([tokens(held, table, m) for m in range(2)], axis=1)
    weight = jnp.concatenate([ref[...] for ref in w_refs], axis=1)
    total = lax.dot_general(grad, weight, (((1,), (1,)), ((), ())), preferred_element_type=F32)
    for ref in y_refs:
        total = total + ref[...]
    total_ref[...] = total
    for i in range(8):
        for h in range(2):
            rows = total_ref[pl.ds(pl.multiple_of(at_ref[i, h], 64), 64), :]
            outs[i][pl.ds(64 * h, 64), :] = rows.astype(outs[i].dtype)


def split(at, first, tiles, pieces, table, gate, lift, ys):
    n = tiles * TILE
    kinds = [F32] + [BF16] * 7
    w = [pl.BlockSpec((256, TILE), lambda j, t=t: (j, first + t)) for t in range(tiles)]
    return pl.pallas_call(
        functools.partial(split_kernel, len(pieces), table, tiles, len(ys)),
        out_shape=tuple(jax.ShapeDtypeStruct((128, 512), t) for t in kinds),
        in_specs=[SMEM]
        + [whole(v.shape) for v in pieces]
        + w
        + w
        + [pl.BlockSpec((1024, 256), lambda j: (0, j))] * len(ys),
        out_specs=tuple(pl.BlockSpec((128, 256), lambda j: (0, j)) for _ in kinds),
        scratch_shapes=[pltpu.VMEM((1024, 256), F32)],
        grid=(2,),
        compiler_params=params(24),
        cost_estimate=cost("k", 4 * 512 * 1024 * n, 8 * 1024 * n + 4 * MIB),
        name="split_rows",
    )(at, *pieces, *[gate] * tiles, *[lift] * tiles, *ys)


class Sequence:
    def __init__(self):
        self.last = None

    def __call__(self, *values):
        if self.last is not None:
            *values, self.last = lax.optimization_barrier((*values, self.last))
        return values[0] if len(values) == 1 else values

    def done(self, value):
        self.last = value


def x_first(seq, first, tiles, use, apart):
    s = {}
    n = tiles * TILE

    def products():
        s["far"], s["near_o"], s["near_k"], s["own"] = forward("a", first, tiles, seq(use["lhs"]), *use["weights"])
        seq.done(s["near_k"])
        s["far"] = over_x(s["far"])

    def relay():
        far, near_k, near_o = seq(s["far"], s["near_k"], s["near_o"])
        near = jnp.stack([(near_k + far.astype(F32)).astype(BF16), near_o])
        seq.done(near)
        s["near"] = over_x(near)

    def swap():
        s["near"] = seq(s["near"])
        other = s["near"][1]
        seq.done(other)
        s["other"] = over_core(other)

    def sum_x():
        near, other, own = seq(s["near"], s["other"], s["own"])
        total = own + near[0].astype(F32) + other.astype(F32)
        send = total[1].astype(BF16)
        seq.done(send)
        s["own"], s["other"] = total[0], over_y(send)

    def gate():
        own, other = seq(s["own"], s["other"])
        use["gated"][first], s["own"] = gating(first, tiles, [own, other], use["cot"])
        seq.done(s["own"])
        s["other"] = over_y(s["own"])

    def spread():
        own, other = seq(s["own"], s["other"])
        s["own"] = jnp.stack([own, other])
        seq.done(s["own"])
        if apart:
            s["near_k"] = over_x(s["own"])
        s["sib"] = over_core(s["own"])

    def spread_x():
        own, sib = seq(s["own"], s["sib"])
        s["full"] = jnp.stack([own, sib])
        seq.done(s["full"])
        if apart:
            s["near_o"] = over_x(sib)
        else:
            s["near"] = over_x(s["full"])

    def pass_on():
        if apart:
            far = s["near_k"] = seq(s["near_k"])
        else:
            s["near"] = seq(s["near"])
            far = s["near"][0]
        seq.done(far)
        s["far"] = over_x(far)

    def swap_near():
        if apart:
            s["held"] = jnp.stack(seq(s["near_k"], s["near_o"], s["far"]))
        else:
            near, far = seq(s["near"], s["far"])
            s["held"] = jnp.concatenate([near, far[None]])
        seq.done(s["held"])
        s["swapped"] = over_core(s["held"])

    def arrived():
        s["swapped"] = seq(s["swapped"])
        seq.done(s["swapped"])

    def pieces():
        return [in_hbm(s[name].reshape(-1, 2, 64, n)) for name in ("full", "held", "swapped")]

    parts = [(0, 0), (1, 0), (1, 1), (1, 2), (0, 1), (2, 0), (2, 1), (2, 2)]
    table = [(i, 2 * j + dy) for dy in range(2) for i, j in parts]
    return dict(
        f=products, a1=relay, ac=swap, a2=sum_x, g=gate, b1=spread, b2=spread_x, b3=pass_on, b4=swap_near, d=arrived,
        pieces=pieces, table=table,
    )


def y_first(seq, first, tiles, use, apart):
    s = {}

    def products():
        s["keep"], send = forward("b", first, tiles, seq(use["lhs"]), *use["weights"])
        seq.done(s["keep"])
        s["other"] = over_y(send)

    def sum_y():
        keep, other = seq(s["keep"], s["other"])
        total = keep + other.astype(F32)
        far = total[0].astype(BF16)
        s["near_o"], s["near_k"], s["own"] = total[1].astype(BF16), total[2], total[3]
        seq.done(far)
        s["far"] = over_x(far)

    def relay():
        far, near_k, near_o = seq(s["far"], s["near_k"], s["near_o"])
        near = jnp.stack([(near_k + far.astype(F32)).astype(BF16), near_o])
        seq.done(near)
        s["near"] = over_x(near)

    def swap():
        s["near"] = seq(s["near"])
        other = s["near"][1]
        seq.done(other)
        s["other"] = over_core(other)

    def gate():
        own, near, other = seq(s["own"], s["near"], s["other"])
        use["gated"][first], s["own"] = gating(first, tiles, [own, near[0], other], use["cot"])
        seq.done(s["own"])
        if apart:
            s["near_k"] = over_x(s["own"])
        s["sib"] = over_core(s["own"])

    def spread_x():
        own, s["sib"] = seq(s["own"], s["sib"])
        if apart:
            seq.done(s["sib"])
            s["near_o"] = over_x(s["sib"])
        else:
            full = jnp.stack([own, s["sib"]])
            seq.done(full)
            s["near"] = over_x(full)

    def pass_on():
        if apart:
            far = s["near_k"] = seq(s["near_k"])
        else:
            s["near"] = seq(s["near"])
            far = s["near"][0]
        seq.done(far)
        s["far"] = over_x(far)

    def collect():
        if apart:
            s["here"] = jnp.stack(seq(s["own"], s["near_k"], s["near_o"], s["far"]))
        else:
            own, near, far = seq(s["own"], s["near"], s["far"])
            s["here"] = jnp.concatenate([own[None], near, far[None]])
        seq.done(s["here"])
        s["there"] = over_y(s["here"])

    def swap_all():
        here, s["there"] = seq(s["here"], s["there"])
        both = jnp.concatenate([here[1:], s["there"]])
        seq.done(both)
        s["swapped"] = over_core(both)

    def arrived():
        s["swapped"] = seq(s["swapped"])
        seq.done(s["swapped"])

    def pieces():
        return [in_hbm(v) for v in (s["here"], s["there"], s["sib"][None], s["swapped"])]

    table = [(0, q) for q in range(4)] + [(2, 0)] + [(3, q) for q in range(3)]
    table += [(1, q) for q in range(4)] + [(3, q) for q in range(3, 7)]
    return dict(
        f=products, b1=sum_y, b2=relay, bc=swap, g=gate, c1=spread_x, c2=pass_on, c3=collect, c4=swap_all, d=arrived,
        pieces=pieces, table=table,
    )


def body(inputs, gate_matrix, lift_matrix, out_cotangent):
    r, c = lax.axis_index("row"), lax.axis_index("col")
    x, yh, k = c // 4, (c // 2) % 2, c % 2

    sib_gate, sib_lift = over_core(gate_matrix), over_core(lift_matrix)
    own_x = lax.all_to_all(jnp.broadcast_to(inputs[None], (8, 128, 512)), "row", 0, 0)
    sib_x = over_core(own_x)

    def block(dx, dy):
        return 2 * ((x + dx) % 4) + (yh + dy) % 2

    fwd = [(2, k), (1 + 2 * k, 1 - k), (1 + 2 * k, k), (0, k)]
    bwd = [(0, k), (3 - 2 * k, k), (3 - 2 * k, 1 - k), (2, k)]
    bwd += [(0, 1 - k), (1 + 2 * k, 1 - k), (1 + 2 * k, k), (2, 1 - k)]
    order = [(block(dx, dy), 64 * h) for dx, h in fwd for dy in range(2)]
    order += [(block(dx, dy), 64 * h) for dy in range(2) for dx, h in bwd]
    at = jnp.stack([jnp.stack([i for i, _ in order]), jnp.stack([h for _, h in order])]).astype(jnp.int32)
    def place(i, h):
        row = (r // 4 + i // 4) % 2 * 4 + (r % 4 + i % 4) % 4
        dx, dy = (row // 2 - x) % 4, (row - yh) % 2
        same = (h == k).astype(jnp.int32)
        near = jnp.where(dx == 3 - 2 * k, 2 - same, 5 + same)
        q = jnp.where(dx == 0, 4 - 4 * same, jnp.where(dx == 2, 7 - 4 * same, near))
        return 64 * (8 * dy + q)

    where = jnp.stack([jnp.stack([place(i, h) for h in range(2)]) for i in range(8)]).astype(jnp.int32)
    at, where = lax.optimization_barrier((at, where))
    lhs = arrange(arrange_kernel, at, own_x, sib_x)

    own_gate, own_lift = in_hbm(gate_matrix), in_hbm(lift_matrix)
    weights = (own_gate, sib_gate, own_lift, sib_lift)
    use = dict(lhs=lhs, weights=weights, cot=out_cotangent, gated={})
    seq = Sequence()
    steps, spans = [], []
    for i, (path, tiles) in enumerate(CHUNKS):
        first = sum(t for j, (_, t) in enumerate(CHUNKS) if (t, j) < (tiles, i))
        steps.append((x_first if path == "a" else y_first)(seq, first, tiles, use, i in APART))
        spans.append((first, tiles))

    grads, ys, xt = None, [], None
    for i, step in ORDER:
        if step == "a2" and xt is None:
            xt = arrange(turn_kernel, at, seq(own_x))
            seq.done(xt)
        if step[0] != "K":
            steps[i][step]()
            if step == "g" and len(use["gated"]) == len(CHUNKS):
                gated = jnp.concatenate([use["gated"][first] for first in sorted(use["gated"])], axis=1)
                seq.done(gated)
            continue
        pieces = steps[i]["pieces"]()
        table = steps[i]["table"]
        if step == "Ky":
            assert len(ys) == len(CHUNKS) - 1
            parts = split(where, *spans[i], pieces, table, own_gate, own_lift, ys)
            got = {i: lax.ppermute(parts[i], "row", row_step(i)) for i in (6, 2, 5, 7, 1, 3, 4)}
            got[6], got[2] = seq(got[6], got[2])
            seq.done(got[2])
            continue
        grads = backward(*spans[i], pieces, table, xt, own_gate, own_lift, grads, step == "K")
        if step == "K":
            seq.done(grads[2])
            ys.append(grads[2])

    total = parts[0]
    for i in range(1, 8):
        total = total + got[i].astype(F32)
    return (gated, total.astype(BF16), grads[0], grads[1])


def solution(mesh):
    return jax.shard_map(
        body,
        mesh=mesh,
        in_specs=(P("row", "col"), P("col", "row"), P("col", "row"), P("col", "row")),
        out_specs=(P("col", "row"), P("row", "col"), P("col", "row"), P("col", "row")),
        check_vma=False,
    )
```

```python
import functools

import jax
import jax.numpy as jnp
from jax import lax
from jax.experimental import pallas as pl
from jax.experimental.pallas import tpu as pltpu
from jax.sharding import PartitionSpec as P

F32, BF16 = jnp.float32, jnp.bfloat16
TILE = 256
CHUNKS = (('b', 3), ('a', 4), ('a', 3), ('a', 3))
ORDER = ((2, 'f'), (3, 'f'), (2, 'a1'), (0, 'f'), (3, 'a1'), (1, 'f'), (2, 'ac'), (0, 'b1'), (3, 'ac'), (2, 'a2'), (1, 'a1'), (3, 'a2'), (2, 'g'), (0, 'b2'), (2, 'b1'), (3, 'g'), (1, 'ac'), (2, 'b2'), (0, 'bc'), (1, 'a2'), (0, 'g'), (0, 'c1'), (1, 'g'), (3, 'b1'), (2, 'b3'), (0, 'c2'), (2, 'b4'), (3, 'b2'), (0, 'c3'), (1, 'b1'), (1, 'b2'), (2, 'd'), (2, 'K'), (3, 'b3'), (0, 'c4'), (1, 'b3'), (3, 'b4'), (0, 'd'), (0, 'K'), (3, 'd'), (1, 'b4'), (3, 'K'), (1, 'd'), (1, 'Ky'), (1, 'Kw'))
MIB = 1 << 20
APART = ()
COST = {'f': 0, 'g': 0.001, 'k': 0.3}


def column(x, y, core):
    return (x % 4) * 4 + (y % 2) * 2 + core % 2


COLS = [(c, c // 4, (c // 2) % 2, c % 2) for c in range(16)]
CORE = [(c, column(x, y, k + 1)) for c, x, y, k in COLS]
ALONG_Y = [(c, column(x, y + 1, k)) for c, x, y, k in COLS]
ALONG_X = [(c, column(x + 1 - 2 * k, y, k)) for c, x, y, k in COLS]


def row_step(i):
    return [(r, ((r // 4 + i // 4) % 2) * 4 + (r % 4 + i % 4) % 4) for r in range(8)]


def over_x(v):
    return lax.ppermute(v, "col", ALONG_X)


def over_y(v):
    return lax.ppermute(v, "col", ALONG_Y)


def over_core(v):
    return lax.ppermute(v, "col", CORE)


def params(mib):
    return pltpu.CompilerParams(vmem_limit_bytes=mib * MIB)


def in_hbm(v):
    return pltpu.with_memory_space_constraint(v, pltpu.HBM)


def whole(shape):
    return pl.BlockSpec(shape, lambda *_: (0,) * len(shape), pipeline_mode=pl.Buffered(1))


SMEM = pl.BlockSpec(memory_space=pltpu.SMEM)
ANY = pl.BlockSpec(memory_space=pl.ANY)


def cost(kind, flops, bytes_accessed):
    part = COST[kind]
    return pl.CostEstimate(flops=int(flops * part), bytes_accessed=int(bytes_accessed * part), transcendentals=0)


def piece(at_ref, ref, i):
    return ref[at_ref[0, i], pl.ds(pl.multiple_of(at_ref[1, i], 64), 64), :]


def arrange_kernel(at_ref, own_ref, sib_ref, lhs_ref):
    for i in range(8):
        lhs_ref[pl.ds(64 * i, 64), :512] = piece(at_ref, own_ref, i)
        lhs_ref[pl.ds(64 * i, 64), 512:] = piece(at_ref, sib_ref, i)


def turn_kernel(at_ref, own_ref, xt_ref):
    for i in range(8):
        pair = [piece(at_ref, own_ref, 8 + 2 * i), piece(at_ref, own_ref, 9 + 2 * i)]
        xt_ref[:, pl.ds(128 * i, 128)] = jnp.concatenate(pair, axis=0).T


def arrange(kernel, at, *blocks):
    return pl.pallas_call(
        kernel,
        out_shape=jax.ShapeDtypeStruct((512, 1024), BF16),
        in_specs=[SMEM] + [whole(v.shape) for v in blocks],
        out_specs=pl.BlockSpec((512, 1024), lambda j: (0, 0)),
        grid=(1,),
        compiler_params=params(8),
        cost_estimate=cost("f", 0, 4 * MIB),
        name="arrange_tokens",
    )(at, *blocks)


def forward_kernel(path, lhs_ref, go_ref, gs_ref, lo_ref, ls_ref, *outs):
    a, b = lhs_ref[:, :512], lhs_ref[:, 512:]
    for m, (o, s) in enumerate(((go_ref, gs_ref), (lo_ref, ls_ref))):
        p = jnp.dot(a, o[...], preferred_element_type=F32)
        p = p + jnp.dot(b, s[...], preferred_element_type=F32)
        for g in range(4):
            for dy in range(2):
                q = p[g * 128 + dy * 64 : g * 128 + dy * 64 + 64]
                if path == "a":
                    outs[g][dy, m] = q.astype(outs[g].dtype)
                else:
                    outs[dy][g, m] = q.astype(outs[dy].dtype)


def forward(path, first, tiles, lhs, own_gate, sib_gate, own_lift, sib_lift):
    n = tiles * TILE
    if path == "a":
        lead, kinds = 2, (BF16, BF16, F32, F32)
    else:
        lead, kinds = 4, (F32, BF16)
    w = pl.BlockSpec((512, TILE), lambda j: (0, first + j))
    return pl.pallas_call(
        functools.partial(forward_kernel, path),
        out_shape=tuple(jax.ShapeDtypeStruct((lead, 2, 64, n), t) for t in kinds),
        in_specs=[whole((512, 1024)), w, w, w, w],
        out_specs=tuple(pl.BlockSpec((lead, 2, 64, TILE), lambda j: (0, 0, 0, j)) for _ in kinds),
        grid=(tiles,),
        compiler_params=params(12),
        cost_estimate=cost("f", 4 * 512 * 1024 * n, 4 * 1024 * n + 6 * 1024 * n),
        name="forward_" + path,
    )(lhs, own_gate, sib_gate, own_lift, sib_lift)


def gate_kernel(terms, *refs):
    total = refs[0][...].astype(F32)
    for ref in refs[1:terms]:
        total = total + ref[...].astype(F32)
    cot = refs[terms][...].astype(F32)
    gated_ref, grads_ref = refs[-2:]
    gate, lift = total[0], total[1]
    sigma = jax.nn.sigmoid(gate)
    silu = gate * sigma
    gated_ref[...] = (silu * lift).astype(BF16)
    grads_ref[0] = (cot * lift * sigma * (1.0 + gate * (1.0 - sigma))).astype(BF16)
    grads_ref[1] = (cot * silu).astype(BF16)


def gating(first, tiles, terms, cot):
    n = tiles * TILE
    return pl.pallas_call(
        functools.partial(gate_kernel, len(terms)),
        out_shape=(jax.ShapeDtypeStruct((64, n), BF16), jax.ShapeDtypeStruct((2, 64, n), BF16)),
        in_specs=[whole((2, 64, n))] * len(terms) + [whole((64, n))],
        out_specs=(pl.BlockSpec((64, n), lambda j: (0, 0)), pl.BlockSpec((2, 64, n), lambda j: (0, 0, 0))),
        grid=(1,),
        compiler_params=params(8),
        cost_estimate=cost("g", 0, 64 * n * 20),
        name="gating",
    )(*terms, cot[:, first * TILE : first * TILE + n])


def tokens(held, table, m):
    return jnp.concatenate([held[i][j, m] for i, j in table], axis=0)


def backward_kernel(arrays, table, with_y, *refs):
    held, xt_ref = refs[:arrays], refs[arrays]
    outs = refs[-3:] if with_y else refs[-2:]
    both = [tokens(held, table, m) for m in range(2)]
    for m in range(2):
        outs[m][...] = jnp.dot(xt_ref[...], both[m], preferred_element_type=F32).astype(BF16)
    if with_y:
        gate_ref, lift_ref = refs[arrays + 1 : arrays + 3]
        grad = jnp.concatenate(both, axis=1)
        weight = jnp.concatenate([gate_ref[...], lift_ref[...]], axis=1)
        part = lax.dot_general(grad, weight, (((1,), (1,)), ((), ())), preferred_element_type=F32)

        @pl.when(pl.program_id(0) == 0)
        def _():
            outs[2][...] = part

        @pl.when(pl.program_id(0) > 0)
        def _():
            outs[2][...] += part


def backward(first, tiles, pieces, table, xt, gate, lift, grads, with_y):
    once = first % tiles == 0
    n = tiles * TILE if once else TILE
    mode = dict(pipeline_mode=pl.Buffered(1)) if once else {}
    wide = pl.BlockSpec((512, n), lambda j: (0, first // tiles if once else first + j), **mode)
    args = [*pieces, xt, gate, lift] if with_y else [*pieces, xt]
    specs = [pl.BlockSpec((v.shape[0], 2, 64, n), lambda j: (0, 0, 0, j), **mode) for v in pieces]
    specs += [whole(xt.shape), wide, wide] if with_y else [whole(xt.shape)]
    alias, shapes = {}, [jax.ShapeDtypeStruct(gate.shape, BF16)] * 2
    column = pl.BlockSpec((512, n), lambda j: (0, first // tiles if once else first + j))
    out_specs = [column, column]
    if with_y:
        shapes.append(jax.ShapeDtypeStruct((1024, 512), F32))
        out_specs.append(pl.BlockSpec((1024, 512), lambda j: (0, 0)))
    if grads is not None:
        for m in range(2):
            alias[len(args)] = m
            args.append(grads[m])
            specs.append(ANY)
    return pl.pallas_call(
        functools.partial(backward_kernel, len(pieces), table, with_y),
        out_shape=tuple(shapes),
        in_specs=specs,
        out_specs=tuple(out_specs),
        grid=(1 if once else tiles,),
        input_output_aliases=alias,
        compiler_params=params(28 if once else 16),
        cost_estimate=cost("k", (1 + with_y) * 4 * 512 * 1024 * n * tiles, 8 * 1024 * n * tiles + 4 * MIB),
        name="backward",
    )(*args)


def split_kernel(arrays, table, tiles, others, at_ref, *refs):
    held, w_refs = refs[:arrays], refs[arrays : arrays + 2 * tiles]
    y_refs, outs = refs[arrays + 2 * tiles :][:others], refs[arrays + 2 * tiles + others : -1]
    total_ref = refs[-1]
    grad = jnp.concatenate([tokens(held, table, m) for m in range(2)], axis=1)
    weight = jnp.concatenate([ref[...] for ref in w_refs], axis=1)
    total = lax.dot_general(grad, weight, (((1,), (1,)), ((), ())), preferred_element_type=F32)
    for ref in y_refs:
        total = total + ref[...]
    total_ref[...] = total
    for i in range(8):
        for h in range(2):
            rows = total_ref[pl.ds(pl.multiple_of(at_ref[i, h], 64), 64), :]
            outs[i][pl.ds(64 * h, 64), :] = rows.astype(outs[i].dtype)


def split(at, first, tiles, pieces, table, gate, lift, ys):
    n = tiles * TILE
    kinds = [F32] + [BF16] * 7
    w = [pl.BlockSpec((256, TILE), lambda j, t=t: (j, first + t)) for t in range(tiles)]
    return pl.pallas_call(
        functools.partial(split_kernel, len(pieces), table, tiles, len(ys)),
        out_shape=tuple(jax.ShapeDtypeStruct((128, 512), t) for t in kinds),
        in_specs=[SMEM]
        + [whole(v.shape) for v in pieces]
        + w
        + w
        + [pl.BlockSpec((1024, 256), lambda j: (0, j))] * len(ys),
        out_specs=tuple(pl.BlockSpec((128, 256), lambda j: (0, j)) for _ in kinds),
        scratch_shapes=[pltpu.VMEM((1024, 256), F32)],
        grid=(2,),
        compiler_params=params(24),
        cost_estimate=cost("k", 4 * 512 * 1024 * n, 8 * 1024 * n + 4 * MIB),
        name="split_rows",
    )(at, *pieces, *[gate] * tiles, *[lift] * tiles, *ys)


class Sequence:
    def __init__(self):
        self.last = None

    def __call__(self, *values):
        if self.last is not None:
            *values, self.last = lax.optimization_barrier((*values, self.last))
        return values[0] if len(values) == 1 else values

    def done(self, value):
        self.last = value


def x_first(seq, first, tiles, use, apart):
    s = {}
    n = tiles * TILE

    def products():
        s["far"], s["near_o"], s["near_k"], s["own"] = forward("a", first, tiles, seq(use["lhs"]), *use["weights"])
        seq.done(s["near_k"])
        s["far"] = over_x(s["far"])

    def relay():
        far, near_k, near_o = seq(s["far"], s["near_k"], s["near_o"])
        near = jnp.stack([(near_k + far.astype(F32)).astype(BF16), near_o])
        seq.done(near)
        s["near"] = over_x(near)

    def swap():
        s["near"] = seq(s["near"])
        other = s["near"][1]
        seq.done(other)
        s["other"] = over_core(other)

    def sum_x():
        near, other, own = seq(s["near"], s["other"], s["own"])
        total = own + near[0].astype(F32) + other.astype(F32)
        send = total[1].astype(BF16)
        seq.done(send)
        s["own"], s["other"] = total[0], over_y(send)

    def gate():
        own, other = seq(s["own"], s["other"])
        use["gated"][first], s["own"] = gating(first, tiles, [own, other], use["cot"])
        seq.done(s["own"])
        s["other"] = over_y(s["own"])

    def spread():
        own, other = seq(s["own"], s["other"])
        s["own"] = jnp.stack([own, other])
        seq.done(s["own"])
        if apart:
            s["near_k"] = over_x(s["own"])
        s["sib"] = over_core(s["own"])

    def spread_x():
        own, sib = seq(s["own"], s["sib"])
        s["full"] = jnp.stack([own, sib])
        seq.done(s["full"])
        if apart:
            s["near_o"] = over_x(sib)
        else:
            s["near"] = over_x(s["full"])

    def pass_on():
        if apart:
            far = s["near_k"] = seq(s["near_k"])
        else:
            s["near"] = seq(s["near"])
            far = s["near"][0]
        seq.done(far)
        s["far"] = over_x(far)

    def swap_near():
        if apart:
            s["held"] = jnp.stack(seq(s["near_k"], s["near_o"], s["far"]))
        else:
            near, far = seq(s["near"], s["far"])
            s["held"] = jnp.concatenate([near, far[None]])
        seq.done(s["held"])
        s["swapped"] = over_core(s["held"])

    def arrived():
        s["swapped"] = seq(s["swapped"])
        seq.done(s["swapped"])

    def pieces():
        return [in_hbm(s[name].reshape(-1, 2, 64, n)) for name in ("full", "held", "swapped")]

    parts = [(0, 0), (1, 0), (1, 1), (1, 2), (0, 1), (2, 0), (2, 1), (2, 2)]
    table = [(i, 2 * j + dy) for dy in range(2) for i, j in parts]
    return dict(
        f=products, a1=relay, ac=swap, a2=sum_x, g=gate, b1=spread, b2=spread_x, b3=pass_on, b4=swap_near, d=arrived,
        pieces=pieces, table=table,
    )


def y_first(seq, first, tiles, use, apart):
    s = {}

    def products():
        s["keep"], send = forward("b", first, tiles, seq(use["lhs"]), *use["weights"])
        seq.done(s["keep"])
        s["other"] = over_y(send)

    def sum_y():
        keep, other = seq(s["keep"], s["other"])
        total = keep + other.astype(F32)
        far = total[0].astype(BF16)
        s["near_o"], s["near_k"], s["own"] = total[1].astype(BF16), total[2], total[3]
        seq.done(far)
        s["far"] = over_x(far)

    def relay():
        far, near_k, near_o = seq(s["far"], s["near_k"], s["near_o"])
        near = jnp.stack([(near_k + far.astype(F32)).astype(BF16), near_o])
        seq.done(near)
        s["near"] = over_x(near)

    def swap():
        s["near"] = seq(s["near"])
        other = s["near"][1]
        seq.done(other)
        s["other"] = over_core(other)

    def gate():
        own, near, other = seq(s["own"], s["near"], s["other"])
        use["gated"][first], s["own"] = gating(first, tiles, [own, near[0], other], use["cot"])
        seq.done(s["own"])
        if apart:
            s["near_k"] = over_x(s["own"])
        s["sib"] = over_core(s["own"])

    def spread_x():
        own, s["sib"] = seq(s["own"], s["sib"])
        if apart:
            seq.done(s["sib"])
            s["near_o"] = over_x(s["sib"])
        else:
            full = jnp.stack([own, s["sib"]])
            seq.done(full)
            s["near"] = over_x(full)

    def pass_on():
        if apart:
            far = s["near_k"] = seq(s["near_k"])
        else:
            s["near"] = seq(s["near"])
            far = s["near"][0]
        seq.done(far)
        s["far"] = over_x(far)

    def collect():
        if apart:
            s["here"] = jnp.stack(seq(s["own"], s["near_k"], s["near_o"], s["far"]))
        else:
            own, near, far = seq(s["own"], s["near"], s["far"])
            s["here"] = jnp.concatenate([own[None], near, far[None]])
        seq.done(s["here"])
        s["there"] = over_y(s["here"])

    def swap_all():
        here, s["there"] = seq(s["here"], s["there"])
        both = jnp.concatenate([here[1:], s["there"]])
        seq.done(both)
        s["swapped"] = over_core(both)

    def arrived():
        s["swapped"] = seq(s["swapped"])
        seq.done(s["swapped"])

    def pieces():
        return [in_hbm(v) for v in (s["here"], s["there"], s["sib"][None], s["swapped"])]

    table = [(0, q) for q in range(4)] + [(2, 0)] + [(3, q) for q in range(3)]
    table += [(1, q) for q in range(4)] + [(3, q) for q in range(3, 7)]
    return dict(
        f=products, b1=sum_y, b2=relay, bc=swap, g=gate, c1=spread_x, c2=pass_on, c3=collect, c4=swap_all, d=arrived,
        pieces=pieces, table=table,
    )


def body(inputs, gate_matrix, lift_matrix, out_cotangent):
    r, c = lax.axis_index("row"), lax.axis_index("col")
    x, yh, k = c // 4, (c // 2) % 2, c % 2

    sib_gate, sib_lift = over_core(gate_matrix), over_core(lift_matrix)
    own_x = lax.all_to_all(jnp.broadcast_to(inputs[None], (8, 128, 512)), "row", 0, 0)
    sib_x = over_core(own_x)

    def block(dx, dy):
        return 2 * ((x + dx) % 4) + (yh + dy) % 2

    fwd = [(2, k), (1 + 2 * k, 1 - k), (1 + 2 * k, k), (0, k)]
    bwd = [(0, k), (3 - 2 * k, k), (3 - 2 * k, 1 - k), (2, k)]
    bwd += [(0, 1 - k), (1 + 2 * k, 1 - k), (1 + 2 * k, k), (2, 1 - k)]
    order = [(block(dx, dy), 64 * h) for dx, h in fwd for dy in range(2)]
    order += [(block(dx, dy), 64 * h) for dy in range(2) for dx, h in bwd]
    at = jnp.stack([jnp.stack([i for i, _ in order]), jnp.stack([h for _, h in order])]).astype(jnp.int32)
    def place(i, h):
        row = (r // 4 + i // 4) % 2 * 4 + (r % 4 + i % 4) % 4
        dx, dy = (row // 2 - x) % 4, (row - yh) % 2
        same = (h == k).astype(jnp.int32)
        near = jnp.where(dx == 3 - 2 * k, 2 - same, 5 + same)
        q = jnp.where(dx == 0, 4 - 4 * same, jnp.where(dx == 2, 7 - 4 * same, near))
        return 64 * (8 * dy + q)

    where = jnp.stack([jnp.stack([place(i, h) for h in range(2)]) for i in range(8)]).astype(jnp.int32)
    at, where = lax.optimization_barrier((at, where))
    lhs = arrange(arrange_kernel, at, own_x, sib_x)

    own_gate, own_lift = in_hbm(gate_matrix), in_hbm(lift_matrix)
    weights = (own_gate, sib_gate, own_lift, sib_lift)
    use = dict(lhs=lhs, weights=weights, cot=out_cotangent, gated={})
    seq = Sequence()
    steps, spans = [], []
    for i, (path, tiles) in enumerate(CHUNKS):
        first = sum(t for j, (_, t) in enumerate(CHUNKS) if (t, j) < (tiles, i))
        steps.append((x_first if path == "a" else y_first)(seq, first, tiles, use, i in APART))
        spans.append((first, tiles))

    grads, ys, xt = None, [], None
    for i, step in ORDER:
        if step == "a2" and xt is None:
            xt = arrange(turn_kernel, at, seq(own_x))
            seq.done(xt)
        if step[0] != "K":
            steps[i][step]()
            if step == "g" and len(use["gated"]) == len(CHUNKS):
                gated = jnp.concatenate([use["gated"][first] for first in sorted(use["gated"])], axis=1)
                seq.done(gated)
            continue
        pieces = steps[i]["pieces"]()
        table = steps[i]["table"]
        if step == "Ky":
            assert len(ys) == len(CHUNKS) - 1
            parts = split(where, *spans[i], pieces, table, own_gate, own_lift, ys)
            got = {i: lax.ppermute(parts[i], "row", row_step(i)) for i in (6, 2, 5, 7, 1, 3, 4)}
            got[6], got[2] = seq(got[6], got[2])
            seq.done(got[2])
            continue
        grads = backward(*spans[i], pieces, table, xt, own_gate, own_lift, grads, step == "K")
        if step == "K":
            seq.done(grads[2])
            ys.append(grads[2])

    total = parts[0]
    for i in range(1, 8):
        total = total + got[i].astype(F32)
    return (gated, total.astype(BF16), grads[0], grads[1])


def solution(mesh):
    return jax.shard_map(
        body,
        mesh=mesh,
        in_specs=(P("row", "col"), P("col", "row"), P("col", "row"), P("col", "row")),
        out_specs=(P("col", "row"), P("row", "col"), P("col", "row"), P("col", "row")),
        check_vma=False,
    )
```
